256 devices in a mesh: ctx: 16 (over x, y), head: 4 (over z_hi), dp: 4 (over z_lo, core).
Axes of the slice: x: 4, y: 4, z: 8 (z_hi: 4, z_lo: 2; z = z_hi * 2 + z_lo), core: 2. Of those that a mesh axis runs over, the one named last changes fastest.
Arguments:
- query_nope: bfloat16 [4, 2048, 4096], P('dp', 'ctx', 'head'), may hold values from -6 to 6
- query_rope: bfloat16 [4, 2048, 2048], P('dp', 'ctx', 'head'), may hold values from -8 to 8
- latent: bfloat16 [4, 2048, 512], P('dp', 'ctx'), may hold values from -6 to 6
- rope_key: bfloat16 [4, 2048, 64], P('dp', 'ctx'), may hold values from -8 to 8
- key_up: bfloat16 [512, 4096], P(None, 'head'), may hold values from -0.25 to 0.25
- value_up: bfloat16 [512, 4096], P(None, 'head'), may hold values from -0.25 to 0.25
- grad_out: bfloat16 [4, 2048, 4096], P('dp', 'ctx', 'head'), may hold values from -6 to 6
- group_order: int32 [32], replicated, may hold values from 0 to 31, each once
Outputs:
- latent_grad: bfloat16 [4, 2048, 512], P('dp', 'ctx', 'head')
- key_up_grad: float32 [512, 4096], P(None, 'head')
- value_up_grad: float32 [512, 4096], P(None, 'head')
The draws below stay inside these ranges and needn't reach their ends.
Inputs may be any that keep to these rules, and one draw needn't show every extreme that they name: `group_order`: a permutation of the 32 group numbers.
All inputs are finite; a program needn't handle non-finite values.
Results may differ from the reference program's by a relative error of at most 0.0091.
Values may be sent and summed in bfloat16 or wider, within the bound.
A program may use at most 64 MiB of HBM per device.

```python
import math
import jax
import jax.numpy as jnp
from jax import lax

LATENT = 512
ROPE = 64
HEADS = 32
HEAD_DIM = 128
TOKENS = 2048
SEQS = 4
GROUP = 64
GROUPS = 32


def draw_query_rope(key, part):
    key = jax.random.fold_in(key, 11)
    values = jnp.clip(jax.random.normal(key, (SEQS, TOKENS, HEADS * ROPE), jnp.float32), -4.0, 4.0)
    return values.astype(jnp.bfloat16)


def draw_rope_key(key, part):
    key = jax.random.fold_in(key, 12)
    values = jnp.clip(jax.random.normal(key, (SEQS, TOKENS, ROPE), jnp.float32), -4.0, 4.0)
    return values.astype(jnp.bfloat16)


def block_scale(stream_key, dims, split, smallest, top_value):
    def one(dim, shards_of):
        heights = jax.random.uniform(jax.random.fold_in(jax.random.fold_in(stream_key, 6), dim), (shards_of,), jnp.float32, smallest / len(split), top_value / len(split))
        return jnp.repeat(jnp.exp(heights), dims[dim] // shards_of).reshape((-1,) + (1,) * (len(dims) - dim - 1))

    level = one(*split[0])
    for cut in split[1:]:
        level = level * one(*cut)
    return level


def centred(stream_key, extent, spread, most, split=(), kind=jnp.bfloat16):
    loudness = block_scale(stream_key, extent, split, -0.22, 0.18) if split else 1.0
    values = jax.random.normal(stream_key, extent, jnp.float32) * spread * loudness
    return jnp.minimum(jnp.maximum(values, -most), most).astype(kind)


def setup_inputs(seed: int = 0) -> dict:
    splits = jax.random.split(jax.random.key(seed), 9)
    return {
        "query_nope": centred(splits[0], (SEQS, TOKENS, HEADS * HEAD_DIM), 1.0, 6.0, ((0, 4), (1, 16), (2, 4))),
        "query_rope": draw_query_rope(jax.random.fold_in(splits[8], 71), 0),
        "latent": centred(splits[2], (SEQS, TOKENS, LATENT), 1.0, 6.0, ((0, 4), (1, 16))),
        "rope_key": draw_rope_key(jax.random.fold_in(splits[8], 71), 0),
        "key_up": centred(splits[4], (LATENT, HEADS * HEAD_DIM), LATENT ** -0.5, 0.25, ((1, 4),)),
        "value_up": centred(splits[5], (LATENT, HEADS * HEAD_DIM), LATENT ** -0.5, 0.25, ((1, 4),)),
        "grad_out": centred(splits[6], (SEQS, TOKENS, HEADS * HEAD_DIM), 1.0, 6.0, ((0, 4), (1, 16), (2, 4))),
        "group_order": jax.random.permutation(splits[7], GROUPS).astype(jnp.int32),
    }


def contract(left_side, right_side, left_dim, right_dim):
    return lax.dot_general(left_side, right_side, (((left_dim,), (right_dim,)), ((), ())), preferred_element_type=jnp.float32)

def positions(group_order, row_count, block_rows):
    row_ids = jnp.arange(row_count, dtype=jnp.int32)
    blocks = row_ids // block_rows
    onehot = blocks[:, None] == jnp.arange(group_order.shape[0], dtype=jnp.int32)[None, :]
    starts = lax.optimization_barrier(jnp.sum(jnp.where(onehot, group_order[None, :], 0), axis=1)).astype(jnp.int32)
    return starts * block_rows + row_ids % block_rows

def head_backward(query_nope, query_rope, grad_out, key_up, value_up, latent, rope_key, visible, factor):
    query_lat = contract(query_nope, key_up, 1, 1).astype(jnp.bfloat16)
    scores = (contract(query_lat, latent, 1, 1) + contract(query_rope, rope_key, 1, 1)) * factor
    scores = jnp.where(visible, scores, -jnp.inf)
    largest = lax.optimization_barrier(jnp.max(scores, axis=1, keepdims=True))
    lifted = jnp.exp(scores - largest)
    totals = lax.optimization_barrier(jnp.sum(lifted, axis=1, keepdims=True))
    attn_probs = lifted / totals
    probs_low = attn_probs.astype(jnp.bfloat16)
    out_lat = contract(probs_low, latent, 1, 0)
    out_low = out_lat.astype(jnp.bfloat16)
    grad_lat = contract(grad_out, value_up, 1, 1)
    grad_low = grad_lat.astype(jnp.bfloat16)
    row_dot = lax.optimization_barrier(jnp.sum(grad_lat * out_lat, axis=1, keepdims=True))
    grad_probs = contract(grad_low, latent, 1, 1)
    grad_scores = (attn_probs * (grad_probs - row_dot) * factor).astype(jnp.bfloat16)
    grad_query = contract(grad_scores, latent, 1, 0).astype(jnp.bfloat16)
    latent_part = contract(probs_low, grad_low, 0, 0) + contract(grad_scores, query_lat, 0, 0)
    key_part = contract(grad_query, query_nope, 0, 0)
    value_part = contract(out_low, grad_out, 0, 0)
    return (latent_part, key_part, value_part)

def reference(query_nope, query_rope, latent, rope_key, key_up, value_up, grad_out, group_order):
    factor = 1.0 / math.sqrt(HEAD_DIM + ROPE)
    key_place = positions(group_order, TOKENS, GROUP)
    visible = key_place[None, :] <= key_place[:, None]
    key_heads = key_up.reshape(LATENT, HEADS, HEAD_DIM).transpose(1, 0, 2)
    value_heads = value_up.reshape(LATENT, HEADS, HEAD_DIM).transpose(1, 0, 2)

    def one_sequence(members):
        nope_seq, rope_seq, latent_seq, rkey_seq, grad_seq = members
        nope_heads = nope_seq.reshape(TOKENS, HEADS, HEAD_DIM).transpose(1, 0, 2)
        rope_heads = rope_seq.reshape(TOKENS, HEADS, ROPE).transpose(1, 0, 2)
        grad_heads = grad_seq.reshape(TOKENS, HEADS, HEAD_DIM).transpose(1, 0, 2)

        def one_head(running, head_items):
            nope_h, rope_h, grad_h, key_h, value_h = head_items
            latent_part, key_part, value_part = head_backward(nope_h, rope_h, grad_h, key_h, value_h, latent_seq, rkey_seq, visible, factor)
            return (running + latent_part, (key_part, value_part))
        zero_sum = jnp.zeros((TOKENS, LATENT), jnp.float32)
        latent_sum, parts = lax.scan(one_head, zero_sum, (nope_heads, rope_heads, grad_heads, key_heads, value_heads))
        return (latent_sum, parts[0], parts[1])
    totals, key_parts, value_parts = lax.map(one_sequence, (query_nope, query_rope, latent, rope_key, grad_out))
    latent_grad = totals.astype(jnp.bfloat16)
    key_up_grad = lax.optimization_barrier(jnp.sum(key_parts, axis=0)).transpose(1, 0, 2).reshape(LATENT, HEADS * HEAD_DIM)
    value_up_grad = lax.optimization_barrier(jnp.sum(value_parts, axis=0)).transpose(1, 0, 2).reshape(LATENT, HEADS * HEAD_DIM)
    return (latent_grad, key_up_grad, value_up_grad)
```

```python
import functools
import math

import jax
import jax.numpy as jnp
from jax import lax
from jax.experimental import pallas as pl
from jax.experimental.pallas import tpu as pltpu
from jax.sharding import PartitionSpec as P

HEAD_DIM = 128
GROUP = 64
F32 = jnp.float32
BF16 = jnp.bfloat16
MESH = pl.DeviceIdType.MESH


def dot_nn(left, right):
    return lax.dot_general(left, right, (((1,), (0,)), ((), ())), preferred_element_type=F32)


def dot_nt(left, right):
    return lax.dot_general(left, right, (((1,), (1,)), ((), ())), preferred_element_type=F32)


def mult(value, factor):
    return pl.multiple_of(value * factor, factor)


def kernel(dims, *refs):
    (nx, ny, nh, nz, heads, latent, rope, factor) = dims
    (
        group_ref, lat_ref, rk_ref, qn_ref, qr_ref, ku_ref, vu_ref, go_ref,
        lat_out, key_out, val_out,
        kbuf, lat_t, qn, qr, ku, vu, go, rk,
        q_t, g_t, g_low, score, gprob, prob, dscore,
        bias, peak, total, inv, rdot,
        o_low, gq_low, g_nat, q_nat,
        lsend, l1a, l1b, l2as, l2bs, l2a, l2b, lzs, lzr, lat_v,
        w_own, w_core, w_acc, w1, w1s, w2, w2s, wz, w_out,
        in_sem, out_sem, ag_s, ag_r, l_s, l_r, l2_s, l2_r, lz_s, lz_r,
        wc_s, wc_r, w1_s, w1_r, w2_s, w2_r, wz_s, wz_r,
        vz_s, vz_r, v2_s, v2_r, v1_s, v1_r, vc_s, vc_r,
    ) = refs
    rows = 128
    blocks = nx * ny
    keys = blocks * rows
    cols = heads * HEAD_DIM
    wide = latent + 128
    chunk = ny * rows
    half_lat = latent // 2

    ctx = lax.axis_index("ctx")
    head = lax.axis_index("head")
    dp = lax.axis_index("dp")
    x, y = ctx // ny, lax.rem(ctx, ny)
    zl, core = dp // 2, lax.rem(dp, 2)

    def xs(off):
        return lax.rem(x + off, nx)

    def ys(off):
        return lax.rem(y + off, ny)

    def at_x(off):
        return {"ctx": xs(off) * ny + y}

    def at_y(off):
        return {"ctx": x * ny + ys(off)}

    def at_core():
        return {"dp": zl * 2 + 1 - core}

    def at_z(off):
        return {"dp": lax.rem(zl + off, nz) * 2 + core}

    def at_head(off):
        return {"head": lax.rem(head + off, nh)}

    x_offs = [o for o in (1, nx - 1, 2) if 0 < o < nx]
    x_offs = list(dict.fromkeys(x_offs))
    y_offs = list(dict.fromkeys([o for o in (1, ny - 1, 2) if 0 < o < ny]))
    partners = (
        [at_x(o) for o in x_offs] + [at_y(o) for o in y_offs] + [at_core()]
        + [at_z(o) for o in range(1, nz)] + [at_head(o) for o in range(1, nh)]
    )

    sends = []

    def send(src, dst, ssem, rsem, where):
        copy = pltpu.make_async_remote_copy(
            src_ref=src, dst_ref=dst, send_sem=ssem, recv_sem=rsem,
            device_id=where, device_id_type=MESH,
        )
        copy.start()
        sends.append(copy)

    def arrived(dst, ssem, rsem, where):
        pltpu.make_async_remote_copy(
            src_ref=dst, dst_ref=dst, send_sem=ssem, recv_sem=rsem,
            device_id=where, device_id_type=MESH,
        ).wait_recv()

    barrier = pltpu.get_barrier_semaphore()
    for where in partners:
        pl.semaphore_signal(barrier, inc=1, device_id=where, device_id_type=MESH)

    own_rows = pl.ds(mult(ctx, rows), rows)
    loads = [
        pltpu.make_async_copy(lat_ref, kbuf.at[own_rows, pl.ds(0, latent)], in_sem.at[0]),
        pltpu.make_async_copy(rk_ref, rk, in_sem.at[1]),
        pltpu.make_async_copy(qn_ref, qn, in_sem.at[2]),
        pltpu.make_async_copy(ku_ref, ku, in_sem.at[3]),
        pltpu.make_async_copy(qr_ref, qr, in_sem.at[4]),
        pltpu.make_async_copy(go_ref, go, in_sem.at[5]),
        pltpu.make_async_copy(vu_ref, vu, in_sem.at[6]),
    ]
    for copy in loads:
        copy.start()

    loads[1].wait()
    spread = lax.broadcasted_iota(jnp.int32, (rope, 128), 0)
    lane = lax.broadcasted_iota(jnp.int32, (rope, 128), 1)
    twice = jnp.where(spread == lax.rem(lane, rope), 1.0, 0.0).astype(BF16)
    kbuf[own_rows, pl.ds(latent, 128)] = dot_nn(rk[...], twice).astype(BF16)
    loads[0].wait()
    pl.semaphore_wait(barrier, len(partners))

    part = rows // 2

    def piece(block, half):
        return kbuf.at[pl.ds(pl.multiple_of(block * rows + half * part, part), part)]

    def gather_send(block, half, slot, where):
        send(piece(block, half), piece(block, half), ag_s.at[half, slot], ag_r.at[half, block], where)

    def gather_wait(block, half):
        arrived(piece(block, half), ag_s.at[half, 0], ag_r.at[half, block], at_x(1))

    slot = 0
    for k in range(max(len(x_offs), len(y_offs))):
        gather_send(ctx, 0, slot, at_x(x_offs[k]))
        gather_send(ctx, 1, slot, at_y(y_offs[k]))
        slot += 1
    for k in range(len(x_offs)):
        gather_send(ctx, 0, slot, at_y(y_offs[k]))
        gather_send(ctx, 1, slot, at_x(x_offs[k]))
        slot += 1

    for copy in loads[2:]:
        copy.wait()
    row_id = lax.broadcasted_iota(jnp.int32, (128, 128), 0)
    col_id = lax.broadcasted_iota(jnp.int32, (128, 128), 1)
    eye = row_id == col_id

    def head_cols(h):
        return pl.ds(mult(h, 128), 128)

    def project(h, carry):
        hc = head_cols(h)
        q_t[pl.ds(0, latent), hc] = dot_nt(ku[:, hc], qn[:, hc]).astype(BF16)
        pick = jnp.where(eye & (row_id // rope == lax.rem(h, 2)), 1.0, 0.0).astype(BF16)
        pair = qr[:, pl.ds(mult(h // 2, 128), 128)]
        q_t[pl.ds(latent, 128), hc] = dot_nt(pick, pair).astype(BF16)
        grad = dot_nt(vu[:, hc], go[:, hc])
        g_t[:, hc] = grad
        g_low[:, hc] = grad.astype(BF16)
        return carry

    lax.fori_loop(0, heads, project, 0)

    for k in range(len(x_offs)):
        block = xs(x_offs[k]) * ny + y
        gather_wait(block, 0)
        for o in y_offs:
            gather_send(block, 0, slot + k * len(y_offs) + y_offs.index(o), at_y(o))
        block = x * ny + ys(y_offs[k])
        gather_wait(block, 1)
        for o in x_offs:
            gather_send(block, 1, slot + k * len(x_offs) + x_offs.index(o), at_x(o))

    lanes = lax.broadcasted_iota(jnp.int32, (GROUP, 128), 1)
    downs = lax.broadcasted_iota(jnp.int32, (GROUP, 128), 0)
    own_low, own_high = group_ref[2 * ctx], group_ref[2 * ctx + 1]
    q_pos = jnp.where(lanes < GROUP, own_low * GROUP + lanes, own_high * GROUP + lanes - GROUP)
    peak[...] = jnp.full(peak.shape, -jnp.inf, F32)
    ident_r = lax.broadcasted_iota(jnp.int32, (latent, latent), 0)
    ident_c = lax.broadcasted_iota(jnp.int32, (latent, latent), 1)
    tile = 256
    tiles = cols // tile

    def tile_cols(n):
        return pl.ds(mult(n, tile), tile)

    for i in range(nx):
        xc = xs(([0] + x_offs)[i])
        for o in range(ny):
            block = xc * ny + ys(o)
            if o > 0:
                gather_wait(block, 0)
            if i > 0:
                gather_wait(block, 1)
        span = pl.ds(mult(xc, chunk), chunk)
        for b in range(ny):
            for g in range(2):
                k_pos = group_ref[2 * (xc * ny + b) + g] * GROUP + downs
                bias[pl.ds(b * rows + g * GROUP, GROUP), :] = jnp.where(k_pos <= q_pos, 0.0, -jnp.inf)

        def one_tile(n, carry, span=span):
            tc = tile_cols(n)
            s = dot_nn(kbuf[span, :], q_t[:, tc])
            mask = bias[...]
            s = s + jnp.concatenate([mask] * (tile // 128), axis=1)
            score[span, tc] = s
            peak[:, tc] = jnp.maximum(peak[:, tc], jnp.max(s, axis=0, keepdims=True))
            gprob[span, tc] = dot_nn(kbuf[span, pl.ds(0, latent)], g_low[:, tc])
            return carry

        lax.fori_loop(0, tiles, one_tile, 0)
        ident = jnp.where(ident_r == ident_c, 1.0, 0.0).astype(BF16)
        lat_t[:, span] = dot_nt(ident, kbuf[span, pl.ds(0, latent)]).astype(BF16)

    step = 256
    steps = keys // step
    total[...] = jnp.zeros(total.shape, F32)
    scale = factor * math.log2(math.e)

    def soften(i, carry):
        span = pl.ds(mult(i, step), step)
        p = jnp.exp2((score[span, :] - peak[...]) * scale)
        total[...] += jnp.sum(p, axis=0, keepdims=True)
        prob[span, :] = p.astype(BF16)
        return carry

    lax.fori_loop(0, steps, soften, 0)
    inv[...] = 1.0 / total[...]

    def read_out(n, carry):
        tc = tile_cols(n)
        o = dot_nn(lat_t[...], prob[:, tc]) * inv[:, tc]
        o_low[:, tc] = o.astype(BF16)
        rdot[:, tc] = jnp.sum(g_t[:, tc] * o, axis=0, keepdims=True)
        return carry

    lax.fori_loop(0, tiles, read_out, 0)

    core_rows = latent // 2
    hw = core_rows // 2

    def chain(w):
        first = ((nx, x, xs, at_x, x_offs), (ny, y, ys, at_y, y_offs))
        base = core * core_rows
        send(
            w_own.at[w, pl.ds(mult(1 - core, core_rows), core_rows)], w_core.at[w],
            wc_s.at[w], wc_r.at[w], at_core(),
        )
        yield
        arrived(w_core.at[w], wc_s.at[w], wc_r.at[w], at_core())
        mine = w_own[w, pl.ds(mult(core, core_rows), core_rows), :].astype(F32)
        w_acc[w] = (mine + w_core[w].astype(F32)).astype(BF16)
        for s in range(2):
            n1, i1, s1, a1, o1 = first[s]
            r = hw // n1
            for o in o1:
                send(
                    w_acc.at[w, pl.ds(pl.multiple_of(s * hw + s1(o) * r, r), r)], w1.at[w, s, o - 1],
                    w1_s.at[w, s, o - 1], w1_r.at[w, s, o - 1], a1(o),
                )
        yield
        for s in range(2):
            n1, i1, s1, a1, o1 = first[s]
            n2, i2, s2, a2, o2 = first[1 - s]
            r = hw // n1
            c = cols // n2
            acc = w_acc[w, pl.ds(pl.multiple_of(s * hw + i1 * r, r), r), :].astype(F32)
            for o in o1:
                arrived(w1.at[w, s, o - 1], w1_s.at[w, s, o - 1], w1_r.at[w, s, o - 1], a1(o))
                acc = acc + w1[w, s, o - 1].astype(F32)
            w1s[w, s] = acc
            for o in o2:
                send(
                    w1s.at[w, s, :, pl.ds(mult(s2(o), c), c)], w2.at[w, s, o - 1],
                    w2_s.at[w, s, o - 1], w2_r.at[w, s, o - 1], a2(o),
                )
        yield
        for s in range(2):
            n1, i1, s1, a1, o1 = first[s]
            n2, i2, s2, a2, o2 = first[1 - s]
            r = hw // n1
            c = cols // n2
            acc = w1s[w, s, :, pl.ds(mult(i2, c), c)]
            for o in o2:
                arrived(w2.at[w, s, o - 1], w2_s.at[w, s, o - 1], w2_r.at[w, s, o - 1], a2(o))
                acc = acc + w2[w, s, o - 1]
            w2s[w, s] = acc
            rz = r // nz
            for o in range(1, nz):
                send(
                    w2s.at[w, s, pl.ds(mult(lax.rem(zl + o, nz), rz), rz)], wz.at[w, s, o - 1],
                    wz_s.at[w, s, o - 1], wz_r.at[w, s, o - 1], at_z(o),
                )
        yield

        def place(s, i1, zi, i2, height, width):
            n1 = first[s][0]
            c = cols // first[1 - s][0]
            r = hw // n1
            top = pl.multiple_of(base + s * hw + i1 * r + zi * (r // nz), r // nz)
            return w_out.at[w, pl.ds(top, height), pl.ds(mult(i2, c), width)]

        for s in range(2):
            n1, i1, s1, a1, o1 = first[s]
            n2, i2, s2, a2, o2 = first[1 - s]
            r = hw // n1
            c = cols // n2
            rz = r // nz
            acc = w2s[w, s, pl.ds(mult(zl, rz), rz), :]
            for o in range(1, nz):
                arrived(wz.at[w, s, o - 1], wz_s.at[w, s, o - 1], wz_r.at[w, s, o - 1], at_z(o))
                acc = acc + wz[w, s, o - 1]
            spot = place(s, i1, zl, i2, rz, c)
            spot[...] = acc.astype(BF16)
            for o in range(1, nz):
                send(spot, spot, vz_s.at[w, s, o - 1], vz_r.at[w, s, o - 1], at_z(o))
        yield
        for s in range(2):
            n1, i1, s1, a1, o1 = first[s]
            n2, i2, s2, a2, o2 = first[1 - s]
            r = hw // n1
            c = cols // n2
            rz = r // nz
            for o in range(1, nz):
                spot = place(s, i1, lax.rem(zl + nz - o, nz), i2, rz, c)
                arrived(spot, vz_s.at[w, s, o - 1], vz_r.at[w, s, o - 1], at_z(o))
            spot = place(s, i1, 0, i2, r, c)
            for o in o2:
                send(spot, spot, v2_s.at[w, s, o - 1], v2_r.at[w, s, o - 1], a2(o))
        yield
        for s in range(2):
            n1, i1, s1, a1, o1 = first[s]
            n2, i2, s2, a2, o2 = first[1 - s]
            r = hw // n1
            c = cols // n2
            for o in o2:
                spot = place(s, i1, 0, s2(n2 - o), r, c)
                arrived(spot, v2_s.at[w, s, o - 1], v2_r.at[w, s, o - 1], a2(o))
            spot = place(s, i1, 0, 0, r, cols)
            for o in o1:
                send(spot, spot, v1_s.at[w, s, o - 1], v1_r.at[w, s, o - 1], a1(o))
        yield
        for s in range(2):
            n1, i1, s1, a1, o1 = first[s]
            r = hw // n1
            for o in o1:
                spot = place(s, s1(n1 - o), 0, 0, r, cols)
                arrived(spot, v1_s.at[w, s, o - 1], v1_r.at[w, s, o - 1], a1(o))
        spot = w_out.at[w, pl.ds(mult(core, core_rows), core_rows)]
        send(spot, spot, vc_s.at[w], vc_r.at[w], at_core())
        yield
        spot = w_out.at[w, pl.ds(mult(1 - core, core_rows), core_rows)]
        arrived(spot, vc_s.at[w], vc_r.at[w], at_core())
        out = pltpu.make_async_copy(w_out.at[w], (val_out, key_out)[w], out_sem.at[w])
        out.start()
        yield
        out.wait()
        yield

    def value_head(h, carry):
        hc = head_cols(h)
        w_own[0, :, hc] = dot_nn(o_low[:, hc], go[:, hc]).astype(BF16)
        return carry

    lax.fori_loop(0, heads, value_head, 0)
    value_chain, key_chain = chain(0), chain(1)
    next(value_chain)

    def rescale(h, carry):
        hc = head_cols(h)
        col = jnp.sum(jnp.where(eye, jnp.broadcast_to(inv[:, hc], (128, 128)), 0.0), axis=1, keepdims=True)
        g_nat[hc, :] = (dot_nt(go[:, hc], vu[:, hc]) * col).astype(BF16)
        q_nat[hc, :] = (dot_nt(qn[:, hc], ku[:, hc]) * (col * factor)).astype(BF16)
        return carry

    lax.fori_loop(0, heads, rescale, 0)

    def grade(i, carry):
        span = pl.ds(mult(i, step), step)
        ds = prob[span, :].astype(F32) * (gprob[span, :] - rdot[...])
        dscore[span, :] = ds.astype(BF16)
        return carry

    lax.fori_loop(0, steps, grade, 0)

    def query_grad(n, carry):
        tc = tile_cols(n)
        gq_low[:, tc] = (dot_nn(lat_t[...], dscore[:, tc]) * (inv[:, tc] * factor)).astype(BF16)
        return carry

    lax.fori_loop(0, tiles, query_grad, 0)

    def key_head(h, carry):
        hc = head_cols(h)
        w_own[1, :, hc] = dot_nn(gq_low[:, hc], qn[:, hc]).astype(BF16)
        return carry

    lax.fori_loop(0, heads, key_head, 0)
    next(key_chain)
    next(value_chain)

    order = x_offs[::-1] + [0]
    for i in range(nx):
        xo = order[i]
        xc = xs(xo)
        span = pl.ds(mult(xc, chunk), chunk)

        def latent_tile(n, carry, span=span):
            cs = pl.ds(mult(n, half_lat), half_lat)
            part_sum = dot_nn(prob[span, :], g_nat[:, cs]) + dot_nn(dscore[span, :], q_nat[:, cs])
            lsend[span, cs] = part_sum.astype(BF16)
            return carry

        lax.fori_loop(0, 2, latent_tile, 0)
        if xo > 0:
            send(
                lsend.at[span, pl.ds(0, half_lat)], l1a.at[xo - 1],
                l_s.at[0, xo - 1], l_r.at[0, xo - 1], at_x(xo),
            )
        for o in y_offs:
            block = pl.ds(mult(xc * ny + ys(o), rows), rows)
            send(
                lsend.at[block, pl.ds(half_lat, half_lat)], l1b.at[o - 1, xc],
                l_s.at[1 + xo, o - 1], l_r.at[1 + xo, o - 1], at_y(o),
            )
        next((key_chain, value_chain)[i % 2])

    for _ in range(2):
        next(key_chain)
        next(value_chain)

    span = pl.ds(mult(x, chunk), chunk)
    acc = lsend[span, pl.ds(0, half_lat)].astype(F32)
    for o in x_offs:
        arrived(l1a.at[o - 1], l_s.at[0, o - 1], l_r.at[0, o - 1], at_x(o))
        acc = acc + l1a[o - 1].astype(F32)
    l2as[...] = acc.astype(BF16)
    for o in y_offs:
        send(
            l2as.at[pl.ds(mult(ys(o), rows), rows)], l2a.at[o - 1],
            l2_s.at[0, o - 1], l2_r.at[0, o - 1], at_y(o),
        )
    for o in y_offs:
        for xo in range(nx):
            arrived(
                l1b.at[o - 1, xs(xo)], l_s.at[1 + xo, o - 1],
                l_r.at[1 + xo, o - 1], at_y(o),
            )
    for xc in range(nx):
        block = pl.ds(mult(xc * ny + y, rows), rows)
        acc = lsend[block, pl.ds(half_lat, half_lat)].astype(F32)
        for o in y_offs:
            acc = acc + l1b[o - 1, xc].astype(F32)
        l2bs[xc] = acc.astype(BF16)
    for o in x_offs:
        send(l2bs.at[xs(o)], l2b.at[o - 1], l2_s.at[1, o - 1], l2_r.at[1, o - 1], at_x(o))
    next(key_chain)
    next(value_chain)

    acc = l2as[pl.ds(mult(y, rows), rows), :].astype(F32)
    for o in y_offs:
        arrived(l2a.at[o - 1], l2_s.at[0, o - 1], l2_r.at[0, o - 1], at_y(o))
        acc = acc + l2a[o - 1].astype(F32)
    lzs[:, pl.ds(0, half_lat)] = acc.astype(BF16)
    acc = l2bs[x].astype(F32)
    for o in x_offs:
        arrived(l2b.at[o - 1], l2_s.at[1, o - 1], l2_r.at[1, o - 1], at_x(o))
        acc = acc + l2b[o - 1].astype(F32)
    lzs[:, pl.ds(half_lat, half_lat)] = acc.astype(BF16)
    share = latent // nh
    for o in range(1, nh):
        send(
            lzs.at[:, pl.ds(mult(lax.rem(head + o, nh), share), share)], lzr.at[o - 1],
            lz_s.at[o - 1], lz_r.at[o - 1], at_head(o),
        )
    next(key_chain)
    next(value_chain)
    acc = lzs[:, pl.ds(mult(head, share), share)].astype(F32)
    for o in range(1, nh):
        arrived(lzr.at[o - 1], lz_s.at[o - 1], lz_r.at[o - 1], at_head(o))
        acc = acc + lzr[o - 1].astype(F32)
    lat_v[...] = acc.astype(BF16)
    out = pltpu.make_async_copy(lat_v, lat_out, out_sem.at[2])
    out.start()
    live = [value_chain, key_chain]
    while live:
        for c in list(live):
            if next(c, "end") == "end":
                live.remove(c)
    out.wait()
    for copy in sends:
        copy.wait_send()


def shards(query_nope, query_rope, latent, rope_key, key_up, value_up, grad_out, group_order):
    ctx, nh, dp = (lax.axis_size(a) for a in ("ctx", "head", "dp"))
    nx = math.isqrt(ctx)
    ny = ctx // nx
    nz = dp // 2
    rows = query_nope.shape[1]
    cols = key_up.shape[1]
    heads = cols // HEAD_DIM
    rope = rope_key.shape[2]
    width = latent.shape[2]
    keys = ctx * rows
    chunk = ny * rows
    half = width // 2
    hw = width // 4
    r1 = hw // nx
    share = width // nh
    factor = 1.0 / math.sqrt(HEAD_DIM + rope)
    dims = (nx, ny, nh, nz, heads, width, rope, factor)
    vmem = pltpu.VMEM
    dma = pltpu.SemaphoreType.DMA
    n3 = max(nx - 1, 1)
    z3 = max(nz - 1, 1)
    h3 = max(nh - 1, 1)
    scratch = [
        vmem((keys, width + 128), BF16),
        vmem((width, keys), BF16),
        vmem((rows, cols), BF16),
        vmem((rows, heads * rope), BF16),
        vmem((width, cols), BF16),
        vmem((width, cols), BF16),
        vmem((rows, cols), BF16),
        vmem((rows, rope), BF16),
        vmem((width + 128, cols), BF16),
        vmem((width, cols), F32),
        vmem((width, cols), BF16),
        vmem((keys, cols), F32),
        vmem((keys, cols), F32),
        vmem((keys, cols), BF16),
        vmem((keys, cols), BF16),
        vmem((chunk, 128), F32),
        vmem((1, cols), F32),
        vmem((1, cols), F32),
        vmem((1, cols), F32),
        vmem((1, cols), F32),
        vmem((width, cols), BF16),
        vmem((width, cols), BF16),
        vmem((cols, width), BF16),
        vmem((cols, width), BF16),
        vmem((keys, width), BF16),
        vmem((n3, chunk, half), BF16),
        vmem((n3, nx, rows, half), BF16),
        vmem((chunk, half), BF16),
        vmem((nx, rows, half), BF16),
        vmem((n3, rows, half), BF16),
        vmem((n3, rows, half), BF16),
        vmem((rows, width), BF16),
        vmem((h3, rows, share), BF16),
        vmem((rows, share), BF16),
        vmem((2, width, cols), BF16),
        vmem((2, width // 2, cols), BF16),
        vmem((2, width // 2, cols), BF16),
        vmem((2, 2, n3, r1, cols), BF16),
        vmem((2, 2, r1, cols), F32),
        vmem((2, 2, n3, r1, cols // ny), F32),
        vmem((2, 2, r1, cols // ny), F32),
        vmem((2, 2, z3, r1 // nz, cols // ny), F32),
        vmem((2, width, cols), BF16),
        dma((7,)), dma((3,)),
        dma((2, 16)), dma((2, ctx)),
        dma((1 + nx, n3)), dma((1 + nx, n3)),
        dma((2, n3)), dma((2, n3)),
        dma((h3,)), dma((h3,)),
        dma((2,)), dma((2,)),
        dma((2, 2, n3)), dma((2, 2, n3)),
        dma((2, 2, n3)), dma((2, 2, n3)),
        dma((2, 2, z3)), dma((2, 2, z3)),
        dma((2, 2, z3)), dma((2, 2, z3)),
        dma((2, 2, n3)), dma((2, 2, n3)),
        dma((2, 2, n3)), dma((2, 2, n3)),
        dma((2,)), dma((2,)),
    ]
    hbm = pl.BlockSpec(memory_space=pl.ANY)
    lat, key_grad, value_grad = pl.pallas_call(
        functools.partial(kernel, dims),
        out_shape=(
            jax.ShapeDtypeStruct((rows, share), BF16),
            jax.ShapeDtypeStruct((width, cols), BF16),
            jax.ShapeDtypeStruct((width, cols), BF16),
        ),
        in_specs=[pl.BlockSpec(memory_space=pltpu.SMEM)] + [hbm] * 7,
        out_specs=(hbm, hbm, hbm),
        scratch_shapes=scratch,
        compiler_params=pltpu.CompilerParams(
            collective_id=0, has_side_effects=True, vmem_limit_bytes=60 * 1024 * 1024
        ),
        cost_estimate=pl.CostEstimate(flops=15_000_000_000, bytes_accessed=8_000_000, transcendentals=2_000_000),
    )(
        group_order, latent[0], rope_key[0], query_nope[0], query_rope[0],
        key_up, value_up, grad_out[0],
    )
    return lat[None], key_grad.astype(F32), value_grad.astype(F32)


def solution(mesh):
    in_specs = (
        P("dp", "ctx", "head"),
        P("dp", "ctx", "head"),
        P("dp", "ctx", None),
        P("dp", "ctx", None),
        P(None, "head"),
        P(None, "head"),
        P("dp", "ctx", "head"),
        P(),
    )
    out_specs = (P("dp", "ctx", "head"), P(None, "head"), P(None, "head"))
    return jax.shard_map(shards, mesh=mesh, in_specs=in_specs, out_specs=out_specs, check_vma=False)
```

```python
import functools
import math

import jax
import jax.numpy as jnp
from jax import lax
from jax.experimental import pallas as pl
from jax.experimental.pallas import tpu as pltpu
from jax.sharding import PartitionSpec as P

HEAD_DIM = 128
GROUP = 64
F32 = jnp.float32
BF16 = jnp.bfloat16
MESH = pl.DeviceIdType.MESH


def dot_nn(left, right):
    return lax.dot_general(left, right, (((1,), (0,)), ((), ())), preferred_element_type=F32)


def dot_nt(left, right):
    return lax.dot_general(left, right, (((1,), (1,)), ((), ())), preferred_element_type=F32)


def dot_tn(left, right):
    return lax.dot_general(left, right, (((0,), (0,)), ((), ())), preferred_element_type=F32)


def mult(value, factor):
    return pl.multiple_of(value * factor, factor)


def kernel(dims, *refs):
    (nx, ny, nh, nz, heads, latent, rope, factor) = dims
    (
        group_ref, lat_ref, rk_ref, qn_ref, qr_ref, ku_ref, vu_ref, go_ref,
        lat_out, key_out, val_out,
        kbuf, lat_t, qn, qr, ku, vu, go, rk,
        q_t, g_t, g_low, score, gprob, prob, dscore,
        bias, peak, peaks, total, inv, rdot,
        o_acc, o_low, gq_low, g_nat, q_nat,
        lsend, l1a, l1b, l2as, l2bs, l2a, l2b, lzs, lzr, lat_v,
        w_own, w_core, w_acc, w1, w1s, w2, w_out,
        in_sem, out_sem, ag_s, ag_r, l_s, l_r, l2_s, l2_r, lz_s, lz_r,
        wc_s, wc_r, w1_s, w1_r, w2_s, w2_r,
        v2_s, v2_r, v1_s, v1_r, vc_s, vc_r, plane,
    ) = refs
    rows = 128
    blocks = nx * ny
    keys = blocks * rows
    cols = heads * HEAD_DIM
    half_lat = latent // 2
    bits = blocks.bit_length() - 1
    chunk = 4 * rows
    chunks = blocks // 4

    ctx = lax.axis_index("ctx")
    head = lax.axis_index("head")
    dp = lax.axis_index("dp")
    zl, core = dp // 2, lax.rem(dp, 2)

    def gray(v):
        return v // 2 * 2 + lax.rem(v // 2 + lax.rem(v, 2), 2)

    def flip(v, off):
        return lax.rem(v // 2 + off // 2, 2) * 2 + lax.rem(lax.rem(v, 2) + off % 2, 2)

    gx, gy = gray(ctx // ny), gray(lax.rem(ctx, ny))

    def block_of(slot):
        return gray(flip(gx, slot // ny)) * ny + gray(flip(gy, slot % ny))

    def at_slot(slot):
        return {"ctx": block_of(slot)}

    def at_x(off):
        return at_slot(off * ny)

    def at_y(off):
        return at_slot(off)

    def at_core():
        return {"dp": zl * 2 + 1 - core}

    def zs(off):
        return lax.rem(zl + off, nz)

    def at_z(off, slot):
        where = {"dp": zs(off) * 2 + core}
        return {**at_slot(slot), **where} if slot else where

    def at_head(off):
        return {"head": lax.rem(head + off, nh)}

    x_offs = list(range(1, nx))
    y_offs = list(range(1, ny))
    partners = (
        [at_slot(1 << t) for t in range(bits)] + [at_core()]
        + [at_z(z, 0) for z in range(1, nz)] + [at_head(o) for o in range(1, nh)]
    )
    order = sorted(range(blocks), key=lambda j: (j.bit_count(), j))
    place_of = {j: i for i, j in enumerate(order)}

    sends = []

    def send(src, dst, ssem, rsem, where):
        copy = pltpu.make_async_remote_copy(
            src_ref=src, dst_ref=dst, send_sem=ssem, recv_sem=rsem,
            device_id=where, device_id_type=MESH,
        )
        copy.start()
        sends.append(copy)

    def arrived(dst, ssem, rsem, where):
        pltpu.make_async_remote_copy(
            src_ref=dst, dst_ref=dst, send_sem=ssem, recv_sem=rsem,
            device_id=where, device_id_type=MESH,
        ).wait_recv()

    barrier = pltpu.get_barrier_semaphore()
    for where in partners:
        pl.semaphore_signal(barrier, inc=1, device_id=where, device_id_type=MESH)

    own_rows = pl.ds(0, rows)
    loads = [
        pltpu.make_async_copy(lat_ref, kbuf.at[own_rows, pl.ds(0, latent)], in_sem.at[0]),
        pltpu.make_async_copy(rk_ref, rk, in_sem.at[1]),
        pltpu.make_async_copy(qn_ref, qn, in_sem.at[2]),
        pltpu.make_async_copy(ku_ref, ku, in_sem.at[3]),
        pltpu.make_async_copy(qr_ref, qr, in_sem.at[4]),
        pltpu.make_async_copy(go_ref, go, in_sem.at[5]),
        pltpu.make_async_copy(vu_ref, vu, in_sem.at[6]),
    ]
    for copy in loads:
        copy.start()

    loads[1].wait()
    spread = lax.broadcasted_iota(jnp.int32, (rope, 128), 0)
    lane = lax.broadcasted_iota(jnp.int32, (rope, 128), 1)
    twice = jnp.where(spread == lax.rem(lane, rope), 1.0, 0.0).astype(BF16)
    kbuf[own_rows, pl.ds(latent, 128)] = dot_tn(rk[...], twice).astype(BF16)
    loads[0].wait()
    pl.semaphore_wait(barrier, len(partners))

    part = rows // bits

    def piece(k, slot):
        return kbuf.at[pl.ds(place_of[slot] * rows + k * part, part)]

    def gather_send(k, slot, step):
        bit = 1 << ((k + step) % bits)
        there = slot ^ bit
        send(piece(k, slot), piece(k, there), ag_s.at[k, there], ag_r.at[k, there], at_slot(bit))

    def last_step(k, slot):
        return max([-1] + [t for t in range(bits) if slot >> ((k + t) % bits) & 1])

    def relay(depth):
        todo = [(last_step(k, j), j, k) for k in range(bits) for j in range(blocks) if j.bit_count() == depth]
        for last, slot, k in sorted(todo):
            arrived(piece(k, slot), ag_s.at[k, slot], ag_r.at[k, slot], at_slot(1))
            for step in range(last + 1, bits):
                gather_send(k, slot, step)

    for step in range(bits):
        for k in range(bits):
            gather_send(k, 0, step)

    for copy in loads[2:]:
        copy.wait()
    row_id = lax.broadcasted_iota(jnp.int32, (128, 128), 0)
    col_id = lax.broadcasted_iota(jnp.int32, (128, 128), 1)
    eye = row_id == col_id

    def head_cols(h):
        return pl.ds(mult(h, 128), 128)

    def project(i, carry):
        for h in (2 * i, 2 * i + 1):
            hc = head_cols(h)
            q_t[pl.ds(0, latent), hc] = dot_nt(ku[:, hc], qn[:, hc]).astype(BF16)
            pick = jnp.where(eye & (row_id // rope == lax.rem(h, 2)), 1.0, 0.0).astype(BF16)
            pair = qr[:, pl.ds(mult(i, 128), 128)]
            q_t[pl.ds(latent, 128), hc] = dot_nt(pick, pair).astype(BF16)
            grad = dot_nt(vu[:, hc], go[:, hc])
            g_t[:, hc] = grad
            g_low[:, hc] = grad.astype(BF16)
        return carry

    lax.fori_loop(0, heads // 2, project, 0)
    relay(1)

    def project_rows(i, carry):
        for h in (2 * i, 2 * i + 1):
            hc = head_cols(h)
            g_nat[hc, :] = dot_nt(go[:, hc], vu[:, hc]).astype(BF16)
            q_nat[hc, :] = (dot_nt(qn[:, hc], ku[:, hc]) * factor).astype(BF16)
        return carry

    lanes = lax.broadcasted_iota(jnp.int32, (GROUP, 128), 1)
    downs = lax.broadcasted_iota(jnp.int32, (GROUP, 128), 0)
    own_low, own_high = group_ref[2 * ctx], group_ref[2 * ctx + 1]
    q_pos = jnp.where(lanes < GROUP, own_low * GROUP + lanes, own_high * GROUP + lanes - GROUP)
    peak[...] = jnp.full(peak.shape, -1e30, F32)
    total[...] = jnp.zeros(total.shape, F32)
    o_acc[...] = jnp.zeros(o_acc.shape, F32)
    ident = jnp.where(eye, 1.0, 0.0).astype(BF16)
    tile = 256
    tiles = cols // tile
    scale = factor * math.log2(math.e)

    def tile_cols(n):
        return pl.ds(mult(n, tile), tile)

    depth = 1
    for i in range(chunks):
        while depth < max(j.bit_count() for j in order[4 * i:4 * i + 4]):
            depth += 1
            relay(depth)
        span = pl.ds(i * chunk, chunk)
        for b in range(4):
            block = block_of(order[4 * i + b])
            for g in range(2):
                k_pos = group_ref[2 * block + g] * GROUP + downs
                bias[pl.ds(b * rows + g * GROUP, GROUP), :] = jnp.where(k_pos <= q_pos, 0.0, -jnp.inf)
        for b in range(latent // 128):
            turned = dot_nt(ident, kbuf[span, pl.ds(b * 128, 128)])
            lat_t[pl.ds(b * 128, 128), span] = turned.astype(BF16)

        def tile_scores(n, span=span):
            return dot_nn(kbuf[span, :], q_t[:, n * tile:(n + 1) * tile])

        s = tile_scores(0)
        for n in range(tiles):
            tc = pl.ds(n * tile, tile)
            ahead = tile_scores(n + 1) if n + 1 < tiles else None
            gprob[span, tc] = dot_nn(kbuf[span, pl.ds(0, latent)], g_low[:, tc])
            s = s + jnp.concatenate([bias[...]] * (tile // 128), axis=1)
            old = peak[:, tc]
            new = jnp.maximum(old, jnp.max(s, axis=0, keepdims=True))
            p = jnp.exp2((s - new) * scale)
            fade = jnp.exp2((old - new) * scale)
            score[span, tc] = p
            total[:, tc] = total[:, tc] * fade + jnp.sum(p, axis=0, keepdims=True)
            peak[:, tc] = new
            peaks[pl.ds(i, 1), tc] = new
            o_acc[:, tc] = o_acc[:, tc] * fade + dot_nn(lat_t[:, span], p.astype(BF16))
            s = ahead
        if i == 0:
            lax.fori_loop(0, heads // 2, project_rows, 0)
        if i + 1 < chunks and depth < bits:
            depth += 1
            relay(depth)

    for z in range(1, nz):
        pl.semaphore_signal(plane, inc=1, device_id=at_z(z, 0), device_id_type=MESH)
    inv[...] = 1.0 / total[...]

    def read_out(n, carry):
        tc = tile_cols(n)
        o = o_acc[:, tc] * inv[:, tc]
        o_low[:, tc] = o.astype(BF16)
        rdot[:, tc] = jnp.sum(g_t[:, tc] * o, axis=0, keepdims=True)
        return carry

    lax.fori_loop(0, tiles, read_out, 0)
    for i in range(chunks):
        peaks[pl.ds(i, 1), :] = jnp.exp2((peaks[pl.ds(i, 1), :] - peak[...]) * scale) * inv[...]

    core_rows = latent // 2
    hw = core_rows // 2

    def chain(w):
        first = ((nx, gx, at_x, x_offs, ny), (ny, gy, at_y, y_offs, 1))
        base = core * core_rows

        def cut(s):
            (n1, i1, a1, o1, u1), (n2, i2, a2, o2, u2) = first[s], first[1 - s]
            pairs = [(o, z) for z in range(nz) for o in range(n2) if o or z]
            return n1, i1, a1, o1, n2, i2, u2, pairs, hw // n1, hw // n1 // nz, cols // n2

        def peer(o, z, u2):
            return at_z(z, o * u2) if z else at_slot(o * u2)

        send(
            w_own.at[w, pl.ds(mult(1 - core, core_rows), core_rows)], w_core.at[w],
            wc_s.at[w], wc_r.at[w], at_core(),
        )
        yield
        arrived(w_core.at[w], wc_s.at[w], wc_r.at[w], at_core())
        mine = w_own[w, pl.ds(mult(core, core_rows), core_rows), :].astype(F32)
        w_acc[w] = (mine + w_core[w].astype(F32)).astype(BF16)
        for s in range(2):
            n1, i1, a1, o1, n2, i2, u2, pairs, r, rz, c = cut(s)
            for o in o1:
                send(
                    w_acc.at[w, pl.ds(pl.multiple_of(s * hw + flip(i1, o) * r, r), r)], w1.at[w, s, o - 1],
                    w1_s.at[w, s, o - 1], w1_r.at[w, s, o - 1], a1(o),
                )
        yield
        for s in range(2):
            n1, i1, a1, o1, n2, i2, u2, pairs, r, rz, c = cut(s)
            acc = w_acc[w, pl.ds(pl.multiple_of(s * hw + i1 * r, r), r), :].astype(F32)
            for o in o1:
                arrived(w1.at[w, s, o - 1], w1_s.at[w, s, o - 1], w1_r.at[w, s, o - 1], a1(o))
                acc = acc + w1[w, s, o - 1].astype(F32)
            w1s[w, s] = acc
            if w == 0 and s == 0 and nz > 1:
                pl.semaphore_wait(plane, nz - 1)
            for o, z in pairs:
                slot = z * n2 + o
                send(
                    w1s.at[w, s, pl.ds(mult(zs(z), rz), rz), pl.ds(mult(flip(i2, o), c), c)],
                    w2.at[w, s, slot], w2_s.at[w, s, slot], w2_r.at[w, s, slot], peer(o, z, u2),
                )
        yield

        def place(s, top, left, height, width):
            start = pl.multiple_of(base + s * hw + top, 16)
            return w_out.at[w, pl.ds(start, height), pl.ds(left, width)]

        for s in range(2):
            n1, i1, a1, o1, n2, i2, u2, pairs, r, rz, c = cut(s)
            acc = w1s[w, s, pl.ds(mult(zl, rz), rz), pl.ds(mult(i2, c), c)]
            for o, z in pairs:
                slot = z * n2 + o
                arrived(w2.at[w, s, slot], w2_s.at[w, s, slot], w2_r.at[w, s, slot], peer(o, z, u2))
                acc = acc + w2[w, s, slot]
            spot = place(s, i1 * r + zl * rz, mult(i2, c), rz, c)
            spot[...] = acc.astype(BF16)
            for o, z in pairs:
                slot = z * n2 + o
                send(spot, spot, v2_s.at[w, s, slot], v2_r.at[w, s, slot], peer(o, z, u2))
        yield
        for s in range(2):
            n1, i1, a1, o1, n2, i2, u2, pairs, r, rz, c = cut(s)
            for o, z in pairs:
                slot = z * n2 + o
                spot = place(s, i1 * r + zs(nz - z) * rz, mult(flip(i2, o), c), rz, c)
                arrived(spot, v2_s.at[w, s, slot], v2_r.at[w, s, slot], peer(o, z, u2))
            spot = place(s, i1 * r, 0, r, cols)
            for o in o1:
                send(spot, spot, v1_s.at[w, s, o - 1], v1_r.at[w, s, o - 1], a1(o))
        yield
        for s in range(2):
            n1, i1, a1, o1, n2, i2, u2, pairs, r, rz, c = cut(s)
            for o in o1:
                spot = place(s, flip(i1, o) * r, 0, r, cols)
                arrived(spot, v1_s.at[w, s, o - 1], v1_r.at[w, s, o - 1], a1(o))
        spot = w_out.at[w, pl.ds(mult(core, core_rows), core_rows)]
        send(spot, spot, vc_s.at[w], vc_r.at[w], at_core())
        yield
        spot = w_out.at[w, pl.ds(mult(1 - core, core_rows), core_rows)]
        arrived(spot, vc_s.at[w], vc_r.at[w], at_core())
        out = pltpu.make_async_copy(w_out.at[w], (val_out, key_out)[w], out_sem.at[w])
        out.start()
        yield
        out.wait()
        yield

    def value_head(h, carry):
        hc = head_cols(h)
        w_own[0, :, hc] = dot_nn(o_low[:, hc], go[:, hc]).astype(BF16)
        return carry

    lax.fori_loop(0, heads, value_head, 0)
    value_chain, key_chain = chain(0), chain(1)
    next(value_chain)

    step = 128

    def grade(j, carry, i=0):
        span = pl.ds(pl.multiple_of(i * chunk + j * step, step), step)
        p = score[span, :] * peaks[pl.ds(i, 1), :]
        prob[span, :] = p.astype(BF16)
        dscore[span, :] = (p * (gprob[span, :] - rdot[...])).astype(BF16)
        return carry

    for i in range(chunks):
        lax.fori_loop(0, chunk // step, functools.partial(grade, i=i), 0)

    def query_grad(n):
        tc = pl.ds(n * tile, tile)
        gq_low[:, tc] = (dot_nn(lat_t[...], dscore[:, tc]) * factor).astype(BF16)

    def key_head(h, carry):
        hc = head_cols(h)
        w_own[1, :, hc] = dot_nn(gq_low[:, hc], qn[:, hc]).astype(BF16)
        return carry

    def latent_chunk(i):
        span = pl.ds(i * chunk, chunk)
        for n in range(2):
            cs = pl.ds(n * half_lat, half_lat)
            part_sum = dot_nn(prob[span, :], g_nat[:, cs]) + dot_nn(dscore[span, :], q_nat[:, cs])
            lsend[span, cs] = part_sum.astype(BF16)
        for slot in reversed(order[4 * i:4 * i + 4]):
            jx, jy = slot // ny, slot % ny
            block = pl.ds(place_of[slot] * rows, rows)
            if jx:
                send(
                    lsend.at[block, pl.ds(0, half_lat)], l1a.at[jx - 1, jy],
                    l_s.at[0, jx - 1, jy], l_r.at[0, jx - 1, jy], at_x(jx),
                )
            if jy:
                send(
                    lsend.at[block, pl.ds(half_lat, half_lat)], l1b.at[jy - 1, jx],
                    l_s.at[1, jy - 1, jx], l_r.at[1, jy - 1, jx], at_y(jy),
                )

    next(value_chain)
    latent_chunk(chunks - 1)
    for n in range(tiles):
        query_grad(n)
    lax.fori_loop(0, heads, key_head, 0)
    next(key_chain)
    next(value_chain)
    rest = list(reversed(range(chunks - 1)))
    for n, i in enumerate(rest):
        latent_chunk(i)
        if n == 0:
            next(key_chain)
        if n == 1:
            next(value_chain)
    for _ in range(2 - len(rest)):
        next((value_chain, key_chain)[_])

    next(key_chain)
    next(value_chain)
    for jy in y_offs + [0]:
        block = pl.ds(place_of[jy] * rows, rows)
        acc = lsend[block, pl.ds(0, half_lat)].astype(F32)
        for jx in x_offs:
            arrived(l1a.at[jx - 1, jy], l_s.at[0, jx - 1, jy], l_r.at[0, jx - 1, jy], at_x(jx))
            acc = acc + l1a[jx - 1, jy].astype(F32)
        l2as[jy] = acc.astype(BF16)
        if jy:
            send(l2as.at[jy], l2a.at[jy - 1], l2_s.at[0, jy - 1], l2_r.at[0, jy - 1], at_y(jy))
    for jx in x_offs + [0]:
        block = pl.ds(place_of[jx * ny] * rows, rows)
        acc = lsend[block, pl.ds(half_lat, half_lat)].astype(F32)
        for jy in y_offs:
            arrived(l1b.at[jy - 1, jx], l_s.at[1, jy - 1, jx], l_r.at[1, jy - 1, jx], at_y(jy))
            acc = acc + l1b[jy - 1, jx].astype(F32)
        l2bs[jx] = acc.astype(BF16)
        if jx:
            send(l2bs.at[jx], l2b.at[jx - 1], l2_s.at[1, jx - 1], l2_r.at[1, jx - 1], at_x(jx))
    next(key_chain)

    acc = l2as[0].astype(F32)
    for o in y_offs:
        arrived(l2a.at[o - 1], l2_s.at[0, o - 1], l2_r.at[0, o - 1], at_y(o))
        acc = acc + l2a[o - 1].astype(F32)
    lzs[:, pl.ds(0, half_lat)] = acc.astype(BF16)
    acc = l2bs[0].astype(F32)
    for o in x_offs:
        arrived(l2b.at[o - 1], l2_s.at[1, o - 1], l2_r.at[1, o - 1], at_x(o))
        acc = acc + l2b[o - 1].astype(F32)
    lzs[:, pl.ds(half_lat, half_lat)] = acc.astype(BF16)
    share = latent // nh
    for o in range(1, nh):
        send(
            lzs.at[:, pl.ds(mult(lax.rem(head + o, nh), share), share)], lzr.at[o - 1],
            lz_s.at[o - 1], lz_r.at[o - 1], at_head(o),
        )
    next(key_chain)
    next(value_chain)
    acc = lzs[:, pl.ds(mult(head, share), share)].astype(F32)
    for o in range(1, nh):
        arrived(lzr.at[o - 1], lz_s.at[o - 1], lz_r.at[o - 1], at_head(o))
        acc = acc + lzr[o - 1].astype(F32)
    lat_v[...] = acc.astype(BF16)
    out = pltpu.make_async_copy(lat_v, lat_out, out_sem.at[2])
    out.start()
    live = [value_chain, key_chain]
    while live:
        for c in list(live):
            if next(c, "end") == "end":
                live.remove(c)
    out.wait()
    for copy in sends:
        copy.wait_send()


def shards(query_nope, query_rope, latent, rope_key, key_up, value_up, grad_out, group_order):
    ctx, nh, dp = (lax.axis_size(a) for a in ("ctx", "head", "dp"))
    nx = math.isqrt(ctx)
    ny = ctx // nx
    nz = dp // 2
    rows = query_nope.shape[1]
    cols = key_up.shape[1]
    heads = cols // HEAD_DIM
    rope = rope_key.shape[2]
    width = latent.shape[2]
    keys = ctx * rows
    bits = ctx.bit_length() - 1
    half = width // 2
    hw = width // 4
    r1 = hw // nx
    share = width // nh
    factor = 1.0 / math.sqrt(HEAD_DIM + rope)
    dims = (nx, ny, nh, nz, heads, width, rope, factor)
    vmem = pltpu.VMEM
    dma = pltpu.SemaphoreType.DMA
    n3 = max(nx - 1, 1)
    h3 = max(nh - 1, 1)
    scratch = [
        vmem((keys, width + 128), BF16),
        vmem((width, keys), BF16),
        vmem((rows, cols), BF16),
        vmem((rows, heads * rope), BF16),
        vmem((width, cols), BF16),
        vmem((width, cols), BF16),
        vmem((rows, cols), BF16),
        vmem((rope, rows), BF16),
        vmem((width + 128, cols), BF16),
        vmem((width, cols), F32),
        vmem((width, cols), BF16),
        vmem((keys, cols), F32),
        vmem((keys, cols), F32),
        vmem((keys, cols), BF16),
        vmem((keys, cols), BF16),
        vmem((512, 128), F32),
        vmem((1, cols), F32),
        vmem((8, cols), F32),
        vmem((1, cols), F32),
        vmem((1, cols), F32),
        vmem((1, cols), F32),
        vmem((width, cols), F32),
        vmem((width, cols), BF16),
        vmem((width, cols), BF16),
        vmem((cols, width), BF16),
        vmem((cols, width), BF16),
        vmem((keys, width), BF16),
        vmem((n3, ny, rows, half), BF16),
        vmem((n3, nx, rows, half), BF16),
        vmem((ny, rows, half), BF16),
        vmem((nx, rows, half), BF16),
        vmem((n3, rows, half), BF16),
        vmem((n3, rows, half), BF16),
        vmem((rows, width), BF16),
        vmem((h3, rows, share), BF16),
        vmem((rows, share), BF16),
        vmem((2, width, cols), BF16),
        vmem((2, width // 2, cols), BF16),
        vmem((2, width // 2, cols), BF16),
        vmem((2, 2, n3, r1, cols), BF16),
        vmem((2, 2, r1, cols), F32),
        vmem((2, 2, ny * nz, r1 // nz, cols // ny), F32),
        vmem((2, width, cols), BF16),
        dma((7,)), dma((3,)),
        dma((bits, ctx)), dma((bits, ctx)),
        dma((2, n3, nx)), dma((2, n3, nx)),
        dma((2, n3)), dma((2, n3)),
        dma((h3,)), dma((h3,)),
        dma((2,)), dma((2,)),
        dma((2, 2, n3)), dma((2, 2, n3)),
        dma((2, 2, ny * nz)), dma((2, 2, ny * nz)),
        dma((2, 2, ny * nz)), dma((2, 2, ny * nz)),
        dma((2, 2, n3)), dma((2, 2, n3)),
        dma((2,)), dma((2,)),
        pltpu.SemaphoreType.REGULAR,
    ]
    hbm = pl.BlockSpec(memory_space=pl.ANY)
    lat, key_grad, value_grad = pl.pallas_call(
        functools.partial(kernel, dims),
        out_shape=(
            jax.ShapeDtypeStruct((rows, share), BF16),
            jax.ShapeDtypeStruct((width, cols), BF16),
            jax.ShapeDtypeStruct((width, cols), BF16),
        ),
        in_specs=[pl.BlockSpec(memory_space=pltpu.SMEM)] + [hbm] * 7,
        out_specs=(hbm, hbm, hbm),
        scratch_shapes=scratch,
        compiler_params=pltpu.CompilerParams(
            collective_id=0, has_side_effects=True, vmem_limit_bytes=60 * 1024 * 1024
        ),
        cost_estimate=pl.CostEstimate(flops=15_000_000_000, bytes_accessed=8_000_000, transcendentals=2_000_000),
    )(
        group_order, latent[0], rope_key[0].T, query_nope[0], query_rope[0],
        key_up, value_up, grad_out[0],
    )
    return lat[None], key_grad.astype(F32), value_grad.astype(F32)


def solution(mesh):
    in_specs = (
        P("dp", "ctx", "head"),
        P("dp", "ctx", "head"),
        P("dp", "ctx", None),
        P("dp", "ctx", None),
        P(None, "head"),
        P(None, "head"),
        P("dp", "ctx", "head"),
        P(),
    )
    out_specs = (P("dp", "ctx", "head"), P(None, "head"), P(None, "head"))
    return jax.shard_map(shards, mesh=mesh, in_specs=in_specs, out_specs=out_specs, check_vma=False)
```

```python
import functools
import math

import jax
import jax.numpy as jnp
from jax import lax
from jax.experimental import pallas as pl
from jax.experimental.pallas import tpu as pltpu
from jax.sharding import PartitionSpec as P

HEAD_DIM = 128
GROUP = 64
F32 = jnp.float32
BF16 = jnp.bfloat16
MESH = pl.DeviceIdType.MESH


def dot_nn(left, right):
    return lax.dot_general(left, right, (((1,), (0,)), ((), ())), preferred_element_type=F32)


def dot_nt(left, right):
    return lax.dot_general(left, right, (((1,), (1,)), ((), ())), preferred_element_type=F32)


def dot_tn(left, right):
    return lax.dot_general(left, right, (((0,), (0,)), ((), ())), preferred_element_type=F32)


def mult(value, factor):
    return pl.multiple_of(value * factor, factor)


def kernel(dims, *refs):
    (nx, ny, nh, nz, heads, latent, rope, factor) = dims
    (
        group_ref, lat_ref, rk_ref, qn_ref, qr_ref, ku_ref, vu_ref, go_ref,
        lat_out, key_out, val_out,
        kbuf, lat_t, qn, qr, ku, vu, go, rk,
        q_t, g_t, g_low, score, gprob, prob, dscore,
        bias, peak, peaks, total, inv, rdot,
        o_acc, o_low, gq_low, g_nat, q_nat,
        lsend, lrecv, lzs, lzr, lat_v,
        w_own, w_core, w_acc, w1, w1s, w2, w_out,
        in_sem, out_sem, ag_s, ag_r, l_s, l_r, lz_s, lz_r,
        wc_s, wc_r, w1_s, w1_r, w2_s, w2_r,
        v2_s, v2_r, v1_s, v1_r, vc_s, vc_r, plane,
    ) = refs
    rows = 128
    blocks = nx * ny
    keys = blocks * rows
    cols = heads * HEAD_DIM
    half_lat = latent // 2
    bits = blocks.bit_length() - 1
    chunk = 4 * rows
    chunks = blocks // 4

    ctx = lax.axis_index("ctx")
    head = lax.axis_index("head")
    dp = lax.axis_index("dp")
    zl, core = dp // 2, lax.rem(dp, 2)

    def gray(v):
        return v // 2 * 2 + lax.rem(v // 2 + lax.rem(v, 2), 2)

    def flip(v, off):
        return lax.rem(v // 2 + off // 2, 2) * 2 + lax.rem(lax.rem(v, 2) + off % 2, 2)

    gx, gy = gray(ctx // ny), gray(lax.rem(ctx, ny))

    def block_of(slot):
        return gray(flip(gx, slot // ny)) * ny + gray(flip(gy, slot % ny))

    def at_slot(slot):
        return {"ctx": block_of(slot)}

    def at_x(off):
        return at_slot(off * ny)

    def at_y(off):
        return at_slot(off)

    def at_core():
        return {"dp": zl * 2 + 1 - core}

    def zs(off):
        return lax.rem(zl + off, nz)

    def at_z(off, slot):
        where = {"dp": zs(off) * 2 + core}
        return {**at_slot(slot), **where} if slot else where

    def at_head(off):
        return {"head": lax.rem(head + off, nh)}

    x_offs = list(range(1, nx))
    y_offs = list(range(1, ny))
    partners = (
        [at_slot(1 << t) for t in range(bits)] + [at_core()]
        + [at_z(z, 0) for z in range(1, nz)] + [at_head(o) for o in range(1, nh)]
    )
    order = sorted(range(blocks), key=lambda j: (j.bit_count(), j))
    place_of = {j: i for i, j in enumerate(order)}

    sends = []

    def send(src, dst, ssem, rsem, where):
        copy = pltpu.make_async_remote_copy(
            src_ref=src, dst_ref=dst, send_sem=ssem, recv_sem=rsem,
            device_id=where, device_id_type=MESH,
        )
        copy.start()
        sends.append(copy)

    def arrived(dst, ssem, rsem, where):
        pltpu.make_async_remote_copy(
            src_ref=dst, dst_ref=dst, send_sem=ssem, recv_sem=rsem,
            device_id=where, device_id_type=MESH,
        ).wait_recv()

    barrier = pltpu.get_barrier_semaphore()
    for where in partners:
        pl.semaphore_signal(barrier, inc=1, device_id=where, device_id_type=MESH)

    own_rows = pl.ds(0, rows)
    loads = [
        pltpu.make_async_copy(lat_ref, kbuf.at[own_rows, pl.ds(0, latent)], in_sem.at[0]),
        pltpu.make_async_copy(rk_ref, rk, in_sem.at[1]),
        pltpu.make_async_copy(qn_ref, qn, in_sem.at[2]),
        pltpu.make_async_copy(ku_ref, ku, in_sem.at[3]),
        pltpu.make_async_copy(qr_ref, qr, in_sem.at[4]),
        pltpu.make_async_copy(go_ref, go, in_sem.at[5]),
        pltpu.make_async_copy(vu_ref, vu, in_sem.at[6]),
    ]
    for copy in loads:
        copy.start()

    loads[1].wait()
    spread = lax.broadcasted_iota(jnp.int32, (rope, 128), 0)
    lane = lax.broadcasted_iota(jnp.int32, (rope, 128), 1)
    twice = jnp.where(spread == lax.rem(lane, rope), 1.0, 0.0).astype(BF16)
    kbuf[own_rows, pl.ds(latent, 128)] = dot_tn(rk[...], twice).astype(BF16)
    loads[0].wait()
    pl.semaphore_wait(barrier, len(partners))

    part = rows // bits

    def piece(k, slot):
        return kbuf.at[pl.ds(place_of[slot] * rows + k * part, part)]

    def gather_send(k, slot, step):
        bit = 1 << ((k + step) % bits)
        there = slot ^ bit
        send(piece(k, slot), piece(k, there), ag_s.at[k, there], ag_r.at[k, there], at_slot(bit))

    def last_step(k, slot):
        return max([-1] + [t for t in range(bits) if slot >> ((k + t) % bits) & 1])

    def relay(depth):
        todo = [(last_step(k, j), j, k) for k in range(bits) for j in range(blocks) if j.bit_count() == depth]
        for last, slot, k in sorted(todo):
            arrived(piece(k, slot), ag_s.at[k, slot], ag_r.at[k, slot], at_slot(1))
            for step in range(last + 1, bits):
                gather_send(k, slot, step)

    for step in range(bits):
        for k in range(bits):
            gather_send(k, 0, step)

    for copy in loads[2:]:
        copy.wait()
    row_id = lax.broadcasted_iota(jnp.int32, (128, 128), 0)
    col_id = lax.broadcasted_iota(jnp.int32, (128, 128), 1)
    eye = row_id == col_id

    def head_cols(h):
        return pl.ds(mult(h, 128), 128)

    def project(i, carry):
        for h in (2 * i, 2 * i + 1):
            hc = head_cols(h)
            q_t[pl.ds(0, latent), hc] = dot_nt(ku[:, hc], qn[:, hc]).astype(BF16)
            pick = jnp.where(eye & (row_id // rope == lax.rem(h, 2)), 1.0, 0.0).astype(BF16)
            pair = qr[:, pl.ds(mult(i, 128), 128)]
            q_t[pl.ds(latent, 128), hc] = dot_nt(pick, pair).astype(BF16)
            grad = dot_nt(vu[:, hc], go[:, hc])
            g_t[:, hc] = grad
            g_low[:, hc] = grad.astype(BF16)
        return carry

    lax.fori_loop(0, heads // 2, project, 0)
    relay(1)

    def project_rows(i, carry):
        for h in (2 * i, 2 * i + 1):
            hc = head_cols(h)
            g_nat[hc, :] = dot_nt(go[:, hc], vu[:, hc]).astype(BF16)
            q_nat[hc, :] = (dot_nt(qn[:, hc], ku[:, hc]) * factor).astype(BF16)
        return carry

    lanes = lax.broadcasted_iota(jnp.int32, (GROUP, 128), 1)
    downs = lax.broadcasted_iota(jnp.int32, (GROUP, 128), 0)
    own_low, own_high = group_ref[2 * ctx], group_ref[2 * ctx + 1]
    q_pos = jnp.where(lanes < GROUP, own_low * GROUP + lanes, own_high * GROUP + lanes - GROUP)
    peak[...] = jnp.full(peak.shape, -1e30, F32)
    total[...] = jnp.zeros(total.shape, F32)
    ident = jnp.where(eye, 1.0, 0.0).astype(BF16)
    tile = 256
    tiles = cols // tile
    scale = factor * math.log2(math.e)

    def tile_cols(n):
        return pl.ds(mult(n, tile), tile)

    depth = 1
    for i in range(chunks):
        while depth < max(j.bit_count() for j in order[4 * i:4 * i + 4]):
            depth += 1
            relay(depth)
        span = pl.ds(i * chunk, chunk)
        for b in range(4):
            block = block_of(order[4 * i + b])
            for g in range(2):
                k_pos = group_ref[2 * block + g] * GROUP + downs
                bias[pl.ds(b * rows + g * GROUP, GROUP), :] = jnp.where(k_pos <= q_pos, 0.0, -jnp.inf)
        for b in range(latent // 128):
            turned = dot_nt(ident, kbuf[span, pl.ds(b * 128, 128)])
            lat_t[pl.ds(b * 128, 128), span] = turned.astype(BF16)

        def tile_scores(n, span=span):
            s = dot_nn(kbuf[span, :], q_t[:, n * tile:(n + 1) * tile])
            return s + jnp.concatenate([bias[...]] * (tile // 128), axis=1)

        score[:, 0:tile] = tile_scores(0)
        for n in range(tiles):
            tc = pl.ds(n * tile, tile)
            if n + 1 < tiles:
                score[:, (n + 1) * tile:(n + 2) * tile] = tile_scores(n + 1)
            gprob[span, tc] = dot_nn(kbuf[span, pl.ds(0, latent)], g_low[:, tc])
            old = peak[:, tc]
            new = jnp.maximum(old, jnp.max(score[:, tc], axis=0, keepdims=True))
            p = jnp.exp2((score[:, tc] - new) * scale)
            prob[span, tc] = p.astype(BF16)
            fade = jnp.exp2((old - new) * scale)
            total[:, tc] = total[:, tc] * fade + jnp.sum(p, axis=0, keepdims=True)
            peak[:, tc] = new
            peaks[pl.ds(i, 1), tc] = new
            o = dot_nn(lat_t[:, span], prob[span, tc])
            o_acc[:, tc] = o if i == 0 else o_acc[:, tc] * fade + o
        if i == 0:
            lax.fori_loop(0, heads // 2, project_rows, 0)
        if i + 1 < chunks and depth < bits:
            depth += 1
            relay(depth)

    for z in range(1, nz):
        pl.semaphore_signal(plane, inc=1, device_id=at_z(z, 0), device_id_type=MESH)
    inv[...] = 1.0 / total[...]

    def read_out(n, carry):
        tc = tile_cols(n)
        o = o_acc[:, tc] * inv[:, tc]
        o_low[:, tc] = o.astype(BF16)
        rdot[:, tc] = jnp.sum(g_t[:, tc] * o, axis=0, keepdims=True)
        return carry

    lax.fori_loop(0, tiles, read_out, 0)
    for i in range(chunks):
        peaks[pl.ds(i, 1), :] = jnp.exp2((peaks[pl.ds(i, 1), :] - peak[...]) * scale) * inv[...]

    core_rows = latent // 2
    hw = core_rows // 2

    def chain(w):
        first = ((nx, gx, at_x, x_offs, ny), (ny, gy, at_y, y_offs, 1))
        base = core * core_rows

        def cut(s):
            (n1, i1, a1, o1, u1), (n2, i2, a2, o2, u2) = first[s], first[1 - s]
            pairs = [(o, z) for z in range(nz) for o in range(n2) if o or z]
            return n1, i1, a1, o1, n2, i2, u2, pairs, hw // n1, hw // n1 // nz, cols // n2

        def peer(o, z, u2):
            return at_z(z, o * u2) if z else at_slot(o * u2)

        send(
            w_own.at[w, pl.ds(mult(1 - core, core_rows), core_rows)], w_core.at[w],
            wc_s.at[w], wc_r.at[w], at_core(),
        )
        yield
        arrived(w_core.at[w], wc_s.at[w], wc_r.at[w], at_core())
        mine = w_own[w, pl.ds(mult(core, core_rows), core_rows), :].astype(F32)
        w_acc[w] = (mine + w_core[w].astype(F32)).astype(BF16)
        for s in range(2):
            n1, i1, a1, o1, n2, i2, u2, pairs, r, rz, c = cut(s)
            for o in o1:
                send(
                    w_acc.at[w, pl.ds(pl.multiple_of(s * hw + flip(i1, o) * r, r), r)], w1.at[w, s, o - 1],
                    w1_s.at[w, s, o - 1], w1_r.at[w, s, o - 1], a1(o),
                )
        yield
        for s in range(2):
            n1, i1, a1, o1, n2, i2, u2, pairs, r, rz, c = cut(s)
            acc = w_acc[w, pl.ds(pl.multiple_of(s * hw + i1 * r, r), r), :].astype(F32)
            for o in o1:
                arrived(w1.at[w, s, o - 1], w1_s.at[w, s, o - 1], w1_r.at[w, s, o - 1], a1(o))
                acc = acc + w1[w, s, o - 1].astype(F32)
            w1s[w, s] = acc
            if w == 0 and s == 0 and nz > 1:
                pl.semaphore_wait(plane, nz - 1)
            for o, z in pairs:
                slot = z * n2 + o
                send(
                    w1s.at[w, s, pl.ds(mult(zs(z), rz), rz), pl.ds(mult(flip(i2, o), c), c)],
                    w2.at[w, s, slot], w2_s.at[w, s, slot], w2_r.at[w, s, slot], peer(o, z, u2),
                )
        yield

        out_ref = (val_out, key_out)[w]

        def to_core(s, o):
            n1, i1, a1, o1, n2, i2, u2, pairs, r, rz, c = cut(s)
            span = pl.ds(pl.multiple_of(base + s * hw + flip(i1, o) * r, 16), r)
            send(w_out.at[w, span], out_ref.at[span], vc_s.at[w, s, o], vc_r.at[w, s, o], at_core())

        def place(s, top, left, height, width):
            start = pl.multiple_of(base + s * hw + top, 16)
            return w_out.at[w, pl.ds(start, height), pl.ds(left, width)]

        for s in range(2):
            n1, i1, a1, o1, n2, i2, u2, pairs, r, rz, c = cut(s)
            acc = w1s[w, s, pl.ds(mult(zl, rz), rz), pl.ds(mult(i2, c), c)]
            for o, z in pairs:
                slot = z * n2 + o
                arrived(w2.at[w, s, slot], w2_s.at[w, s, slot], w2_r.at[w, s, slot], peer(o, z, u2))
                acc = acc + w2[w, s, slot]
            spot = place(s, i1 * r + zl * rz, mult(i2, c), rz, c)
            spot[...] = acc.astype(BF16)
            for o, z in pairs:
                slot = z * n2 + o
                send(spot, spot, v2_s.at[w, s, slot], v2_r.at[w, s, slot], peer(o, z, u2))
        yield
        for s in range(2):
            n1, i1, a1, o1, n2, i2, u2, pairs, r, rz, c = cut(s)
            for o, z in pairs:
                slot = z * n2 + o
                spot = place(s, i1 * r + zs(nz - z) * rz, mult(flip(i2, o), c), rz, c)
                arrived(spot, v2_s.at[w, s, slot], v2_r.at[w, s, slot], peer(o, z, u2))
            spot = place(s, i1 * r, 0, r, cols)
            for o in o1:
                send(spot, spot, v1_s.at[w, s, o - 1], v1_r.at[w, s, o - 1], a1(o))
            to_core(s, 0)
        yield
        for s in range(2):
            n1, i1, a1, o1, n2, i2, u2, pairs, r, rz, c = cut(s)
            for o in o1:
                spot = place(s, flip(i1, o) * r, 0, r, cols)
                arrived(spot, v1_s.at[w, s, o - 1], v1_r.at[w, s, o - 1], a1(o))
                to_core(s, o)
        span = pl.ds(mult(core, core_rows), core_rows)
        own = pltpu.make_async_copy(w_out.at[w, span], out_ref.at[span], out_sem.at[w])
        own.start()
        yield
        for s in range(2):
            n1, i1, a1, o1, n2, i2, u2, pairs, r, rz, c = cut(s)
            for o in [0] + o1:
                span = pl.ds(pl.multiple_of((1 - core) * core_rows + s * hw + flip(i1, o) * r, 16), r)
                arrived(out_ref.at[span], vc_s.at[w, s, o], vc_r.at[w, s, o], at_core())
        own.wait()
        yield

    def value_head(h, carry):
        hc = head_cols(h)
        w_own[0, :, hc] = dot_nn(o_low[:, hc], go[:, hc]).astype(BF16)
        return carry

    lax.fori_loop(0, heads, value_head, 0)
    value_chain, key_chain = chain(0), chain(1)
    next(value_chain)

    step = 128

    def grade(j, carry, i=0):
        span = pl.ds(pl.multiple_of(i * chunk + j * step, step), step)
        p = prob[span, :].astype(F32) * peaks[pl.ds(i, 1), :]
        prob[span, :] = p.astype(BF16)
        dscore[span, :] = (p * (gprob[span, :] - rdot[...])).astype(BF16)
        return carry

    for i in range(chunks):
        lax.fori_loop(0, chunk // step, functools.partial(grade, i=i), 0)

    def query_grad(n):
        tc = pl.ds(n * tile, tile)
        gq_low[:, tc] = (dot_nn(lat_t[...], dscore[:, tc]) * factor).astype(BF16)

    def key_head(h, carry):
        hc = head_cols(h)
        w_own[1, :, hc] = dot_nn(gq_low[:, hc], qn[:, hc]).astype(BF16)
        return carry

    if bits == 4:
        stages = (((0,), (1,), (2, 3)), ((2,), (3,), (0, 1)), ((1,), (0,), (2, 3)), ((3,), (2,), (0, 1)))
    else:
        stages = (((0,), (1,)), ((1,), (0,)), ((0,), (1,)), ((1,), (0,)))
    width = latent // 4
    round_of = {slot: chunks - 1 - place_of[slot] // 4 for slot in range(blocks)}

    def masks(k):
        return [sum(1 << t for t in group) for group in stages[k]]

    def stage_of(k, slot):
        return next((t for t, m in enumerate(masks(k)) if slot & m), len(stages[k]))

    def sources(k, slot):
        return [
            (slot | h, h) for m in masks(k)[:stage_of(k, slot)] for h in range(1, blocks) if h & m == h
        ]

    def ready(k, slot):
        return max([round_of[slot]] + [ready(k, src) + 1 for src, _ in sources(k, slot)])

    def latent_piece(k, slot):
        return lsend.at[pl.ds(place_of[slot] * rows, rows), pl.ds(k * width, width)]

    def latent_sum(k, slot):
        acc = latent_piece(k, slot)[...].astype(F32)
        for src, hop in sources(k, slot):
            arrived(lrecv.at[k, src], l_s.at[k, src], l_r.at[k, src], at_slot(hop))
            acc = acc + lrecv[k, src].astype(F32)
        return acc

    def latent_send(k, slot):
        if sources(k, slot):
            latent_piece(k, slot)[...] = latent_sum(k, slot).astype(BF16)
        hop = slot & masks(k)[stage_of(k, slot)]
        send(latent_piece(k, slot), lrecv.at[k, slot], l_s.at[k, slot], l_r.at[k, slot], at_slot(hop))

    def latent_chunk(n):
        span = pl.ds((chunks - 1 - n) * chunk, chunk)
        for c in range(2):
            cs = pl.ds(c * half_lat, half_lat)
            part_sum = dot_nn(prob[span, :], g_nat[:, cs]) + dot_nn(dscore[span, :], q_nat[:, cs])
            lsend[span, cs] = part_sum.astype(BF16)

    def latent_sends(n):
        todo = [
            (stage_of(k, j), -place_of[j], k, j)
            for j in range(1, blocks) for k in range(4) if min(ready(k, j), chunks - 1) == n
        ]
        for _, _, k, j in sorted(todo):
            latent_send(k, j)

    for n in range(tiles):
        query_grad(n)
    next(value_chain)
    lax.fori_loop(0, heads, key_head, 0)
    next(key_chain)
    latent_chunk(0)
    next(key_chain)
    latent_sends(0)
    if chunks > 1:
        latent_chunk(1)
        next(value_chain)
        latent_sends(1)
        latent_chunk(2)
        latent_sends(2)
        next(key_chain)
        latent_chunk(3)
        next(value_chain)
        latent_sends(3)
    else:
        next(value_chain)
        next(key_chain)
        next(value_chain)
    next(key_chain)
    next(value_chain)
    next(key_chain)
    for k in range(4):
        lzs[:, pl.ds(k * width, width)] = latent_sum(k, 0).astype(BF16)
    share = latent // nh
    for o in range(1, nh):
        send(
            lzs.at[:, pl.ds(mult(lax.rem(head + o, nh), share), share)], lzr.at[o - 1],
            lz_s.at[o - 1], lz_r.at[o - 1], at_head(o),
        )
    next(value_chain)
    next(key_chain)
    acc = lzs[:, pl.ds(mult(head, share), share)].astype(F32)
    for o in range(1, nh):
        arrived(lzr.at[o - 1], lz_s.at[o - 1], lz_r.at[o - 1], at_head(o))
        acc = acc + lzr[o - 1].astype(F32)
    lat_v[...] = acc.astype(BF16)
    out = pltpu.make_async_copy(lat_v, lat_out, out_sem.at[2])
    out.start()
    live = [value_chain, key_chain]
    while live:
        for c in list(live):
            if next(c, "end") == "end":
                live.remove(c)
    out.wait()
    for copy in sends:
        copy.wait_send()


def widen(lat_ref, key_ref, value_ref, lat_out, key_out, value_out):
    lat_out[...] = lat_ref[...]
    key_out[...] = key_ref[...].astype(F32)
    value_out[...] = value_ref[...].astype(F32)


def shards(query_nope, query_rope, latent, rope_key, key_up, value_up, grad_out, group_order):
    ctx, nh, dp = (lax.axis_size(a) for a in ("ctx", "head", "dp"))
    nx = math.isqrt(ctx)
    ny = ctx // nx
    nz = dp // 2
    rows = query_nope.shape[1]
    cols = key_up.shape[1]
    heads = cols // HEAD_DIM
    rope = rope_key.shape[2]
    width = latent.shape[2]
    keys = ctx * rows
    bits = ctx.bit_length() - 1
    hw = width // 4
    r1 = hw // nx
    share = width // nh
    factor = 1.0 / math.sqrt(HEAD_DIM + rope)
    dims = (nx, ny, nh, nz, heads, width, rope, factor)
    vmem = pltpu.VMEM
    dma = pltpu.SemaphoreType.DMA
    n3 = max(nx - 1, 1)
    h3 = max(nh - 1, 1)
    scratch = [
        vmem((keys, width + 128), BF16),
        vmem((width, keys), BF16),
        vmem((rows, cols), BF16),
        vmem((rows, heads * rope), BF16),
        vmem((width, cols), BF16),
        vmem((width, cols), BF16),
        vmem((rows, cols), BF16),
        vmem((rope, rows), BF16),
        vmem((width + 128, cols), BF16),
        vmem((width, cols), F32),
        vmem((width, cols), BF16),
        vmem((512, cols), F32),
        vmem((keys, cols), F32),
        vmem((keys, cols), BF16),
        vmem((keys, cols), BF16),
        vmem((512, 128), F32),
        vmem((1, cols), F32),
        vmem((8, cols), F32),
        vmem((1, cols), F32),
        vmem((1, cols), F32),
        vmem((1, cols), F32),
        vmem((width, cols), F32),
        vmem((width, cols), BF16),
        vmem((width, cols), BF16),
        vmem((cols, width), BF16),
        vmem((cols, width), BF16),
        vmem((keys, width), BF16),
        vmem((4, ctx, rows, width // 4), BF16),
        vmem((rows, width), BF16),
        vmem((h3, rows, share), BF16),
        vmem((rows, share), BF16),
        vmem((2, width, cols), BF16),
        vmem((2, width // 2, cols), BF16),
        vmem((2, width // 2, cols), BF16),
        vmem((2, 2, n3, r1, cols), BF16),
        vmem((2, 2, r1, cols), F32),
        vmem((2, 2, ny * nz, r1 // nz, cols // ny), F32),
        vmem((2, width, cols), BF16),
        dma((7,)), dma((3,)),
        dma((bits, ctx)), dma((bits, ctx)),
        dma((4, ctx)), dma((4, ctx)),
        dma((h3,)), dma((h3,)),
        dma((2,)), dma((2,)),
        dma((2, 2, n3)), dma((2, 2, n3)),
        dma((2, 2, ny * nz)), dma((2, 2, ny * nz)),
        dma((2, 2, ny * nz)), dma((2, 2, ny * nz)),
        dma((2, 2, n3)), dma((2, 2, n3)),
        dma((2, 2, nx)), dma((2, 2, nx)),
        pltpu.SemaphoreType.REGULAR,
    ]
    hbm = pl.BlockSpec(memory_space=pl.ANY)
    lat, key_grad, value_grad = pl.pallas_call(
        functools.partial(kernel, dims),
        out_shape=(
            jax.ShapeDtypeStruct((rows, share), BF16),
            jax.ShapeDtypeStruct((width, cols), BF16),
            jax.ShapeDtypeStruct((width, cols), BF16),
        ),
        in_specs=[pl.BlockSpec(memory_space=pltpu.SMEM)] + [hbm] * 7,
        out_specs=(hbm, hbm, hbm),
        scratch_shapes=scratch,
        compiler_params=pltpu.CompilerParams(
            collective_id=0, has_side_effects=True, vmem_limit_bytes=60 * 1024 * 1024
        ),
        cost_estimate=pl.CostEstimate(flops=15_000_000_000, bytes_accessed=8_000_000, transcendentals=2_000_000),
    )(
        group_order, latent[0], rope_key[0].T, query_nope[0], query_rope[0],
        key_up, value_up, grad_out[0],
    )
    tall = width // 4
    whole = pl.BlockSpec((rows, share), lambda i: (0, 0))
    block = pl.BlockSpec((tall, cols), lambda i: (i, 0))
    lat, key_grad, value_grad = pl.pallas_call(
        widen,
        grid=(width // tall,),
        out_shape=(
            jax.ShapeDtypeStruct((rows, share), BF16),
            jax.ShapeDtypeStruct((width, cols), F32),
            jax.ShapeDtypeStruct((width, cols), F32),
        ),
        in_specs=[whole, block, block],
        out_specs=(whole, block, block),
    )(lat, key_grad, value_grad)
    return lat[None], key_grad, value_grad


def solution(mesh):
    in_specs = (
        P("dp", "ctx", "head"),
        P("dp", "ctx", "head"),
        P("dp", "ctx", None),
        P("dp", "ctx", None),
        P(None, "head"),
        P(None, "head"),
        P("dp", "ctx", "head"),
        P(),
    )
    out_specs = (P("dp", "ctx", "head"), P(None, "head"), P(None, "head"))
    return jax.shard_map(shards, mesh=mesh, in_specs=in_specs, out_specs=out_specs, check_vma=False)
```

```python
import functools
import math

import jax
import jax.numpy as jnp
from jax import lax
from jax.experimental import pallas as pl
from jax.experimental.pallas import tpu as pltpu
from jax.sharding import PartitionSpec as P

HEAD_DIM = 128
GROUP = 64
F32 = jnp.float32
BF16 = jnp.bfloat16
MESH = pl.DeviceIdType.MESH
CUTS = 4
PLAN = ("value", "v", "query", "v", "key", "k", "c0", "k", "v", "c1", "s0", "c2", "k", "v", "s1", "c3", "k", "v", "s2", "s3", "k", "v", "heads", "k", "finish", "v", "k")


def dot_nn(left, right):
    return lax.dot_general(left, right, (((1,), (0,)), ((), ())), preferred_element_type=F32)


def dot_nt(left, right):
    return lax.dot_general(left, right, (((1,), (1,)), ((), ())), preferred_element_type=F32)


def dot_tn(left, right):
    return lax.dot_general(left, right, (((0,), (0,)), ((), ())), preferred_element_type=F32)


def mult(value, factor):
    return pl.multiple_of(value * factor, factor)


def kernel(dims, *refs):
    (nx, ny, nh, nz, heads, latent, rope, factor) = dims
    (
        group_ref, lat_ref, rk_ref, qn_ref, qr_ref, ku_ref, vu_ref, go_ref,
        lat_out, key_out, val_out,
        kbuf, lat_t, qn, qr, ku, vu, go, rk,
        q_t, g_t, g_low, score, gprob, prob, dscore,
        bias, peak, peaks, total, inv, rdot,
        o_acc, o_low, gq_low, g_nat, q_nat,
        lsend, lrecv, lzs, lzr, lat_v,
        w_own, w_core, w_acc, w1, w1s, w2, w_out,
        in_sem, out_sem, ag_s, ag_r, l_s, l_r, lz_s, lz_r,
        wc_s, wc_r, w1_s, w1_r, w2_s, w2_r,
        v2_s, v2_r, v1_s, v1_r, vc_s, vc_r, plane,
    ) = refs
    rows = 128
    blocks = nx * ny
    keys = blocks * rows
    cols = heads * HEAD_DIM
    half_lat = latent // 2
    bits = blocks.bit_length() - 1
    chunk = 4 * rows
    chunks = blocks // 4

    ctx = lax.axis_index("ctx")
    head = lax.axis_index("head")
    dp = lax.axis_index("dp")
    zl, core = dp // 2, lax.rem(dp, 2)

    def gray(v):
        return v // 2 * 2 + lax.rem(v // 2 + lax.rem(v, 2), 2)

    def flip(v, off):
        return lax.rem(v // 2 + off // 2, 2) * 2 + lax.rem(lax.rem(v, 2) + off % 2, 2)

    gx, gy = gray(ctx // ny), gray(lax.rem(ctx, ny))

    def block_of(slot):
        return gray(flip(gx, slot // ny)) * ny + gray(flip(gy, slot % ny))

    def at_slot(slot):
        return {"ctx": block_of(slot)}

    def at_x(off):
        return at_slot(off * ny)

    def at_y(off):
        return at_slot(off)

    def at_core():
        return {"dp": zl * 2 + 1 - core}

    def zs(off):
        return lax.rem(zl + off, nz)

    def at_z(off, slot):
        where = {"dp": zs(off) * 2 + core}
        return {**at_slot(slot), **where} if slot else where

    def at_head(off):
        return {"head": lax.rem(head + off, nh)}

    x_offs = list(range(1, nx))
    y_offs = list(range(1, ny))
    partners = (
        [at_slot(1 << t) for t in range(bits)] + [at_core()]
        + [at_z(z, 0) for z in range(1, nz)] + [at_head(o) for o in range(1, nh)]
    )
    order = sorted(range(blocks), key=lambda j: (j.bit_count(), j))
    place_of = {j: i for i, j in enumerate(order)}

    sends = []

    def send(src, dst, ssem, rsem, where):
        copy = pltpu.make_async_remote_copy(
            src_ref=src, dst_ref=dst, send_sem=ssem, recv_sem=rsem,
            device_id=where, device_id_type=MESH,
        )
        copy.start()
        sends.append(copy)

    def arrived(dst, ssem, rsem, where):
        pltpu.make_async_remote_copy(
            src_ref=dst, dst_ref=dst, send_sem=ssem, recv_sem=rsem,
            device_id=where, device_id_type=MESH,
        ).wait_recv()

    barrier = pltpu.get_barrier_semaphore()
    for where in partners:
        pl.semaphore_signal(barrier, inc=1, device_id=where, device_id_type=MESH)

    own_rows = pl.ds(0, rows)
    loads = [
        pltpu.make_async_copy(lat_ref, kbuf.at[own_rows, pl.ds(0, latent)], in_sem.at[0]),
        pltpu.make_async_copy(rk_ref, rk, in_sem.at[1]),
        pltpu.make_async_copy(qn_ref, qn, in_sem.at[2]),
        pltpu.make_async_copy(ku_ref, ku, in_sem.at[3]),
        pltpu.make_async_copy(qr_ref, qr, in_sem.at[4]),
        pltpu.make_async_copy(go_ref, go, in_sem.at[5]),
        pltpu.make_async_copy(vu_ref, vu, in_sem.at[6]),
    ]
    for copy in loads:
        copy.start()

    loads[1].wait()
    spread = lax.broadcasted_iota(jnp.int32, (rope, 128), 0)
    lane = lax.broadcasted_iota(jnp.int32, (rope, 128), 1)
    twice = jnp.where(spread == lax.rem(lane, rope), 1.0, 0.0).astype(BF16)
    kbuf[own_rows, pl.ds(latent, 128)] = dot_tn(rk[...], twice).astype(BF16)
    loads[0].wait()
    pl.semaphore_wait(barrier, len(partners))

    part = rows // bits

    def piece(k, slot):
        return kbuf.at[pl.ds(place_of[slot] * rows + k * part, part)]

    def gather_send(k, slot, step):
        bit = 1 << ((k + step) % bits)
        there = slot ^ bit
        send(piece(k, slot), piece(k, there), ag_s.at[k, there], ag_r.at[k, there], at_slot(bit))

    def last_step(k, slot):
        return max([-1] + [t for t in range(bits) if slot >> ((k + t) % bits) & 1])

    def relay(depth):
        todo = [(last_step(k, j), j, k) for k in range(bits) for j in range(blocks) if j.bit_count() == depth]
        for last, slot, k in sorted(todo):
            arrived(piece(k, slot), ag_s.at[k, slot], ag_r.at[k, slot], at_slot(1))
            for step in range(last + 1, bits):
                gather_send(k, slot, step)

    for step in range(bits):
        for k in range(bits):
            gather_send(k, 0, step)

    for copy in loads[2:]:
        copy.wait()
    row_id = lax.broadcasted_iota(jnp.int32, (128, 128), 0)
    col_id = lax.broadcasted_iota(jnp.int32, (128, 128), 1)
    eye = row_id == col_id

    def head_cols(h):
        return pl.ds(mult(h, 128), 128)

    def project(i, carry):
        for h in (2 * i, 2 * i + 1):
            hc = head_cols(h)
            q_t[pl.ds(0, latent), hc] = dot_nt(ku[:, hc], qn[:, hc]).astype(BF16)
            pick = jnp.where(eye & (row_id // rope == lax.rem(h, 2)), 1.0, 0.0).astype(BF16)
            pair = qr[:, pl.ds(mult(i, 128), 128)]
            q_t[pl.ds(latent, 128), hc] = dot_nt(pick, pair).astype(BF16)
            grad = dot_nt(vu[:, hc], go[:, hc])
            g_t[:, hc] = grad
            g_low[:, hc] = grad.astype(BF16)
        return carry

    lax.fori_loop(0, heads // 2, project, 0)
    relay(1)

    def project_rows(i, carry):
        for h in (2 * i, 2 * i + 1):
            hc = head_cols(h)
            g_nat[hc, :] = dot_nt(go[:, hc], vu[:, hc]).astype(BF16)
            q_nat[hc, :] = (dot_nt(qn[:, hc], ku[:, hc]) * factor).astype(BF16)
        return carry

    lanes = lax.broadcasted_iota(jnp.int32, (GROUP, 128), 1)
    downs = lax.broadcasted_iota(jnp.int32, (GROUP, 128), 0)
    own_low, own_high = group_ref[2 * ctx], group_ref[2 * ctx + 1]
    q_pos = jnp.where(lanes < GROUP, own_low * GROUP + lanes, own_high * GROUP + lanes - GROUP)
    peak[...] = jnp.full(peak.shape, -1e30, F32)
    total[...] = jnp.zeros(total.shape, F32)
    ident = jnp.where(eye, 1.0, 0.0).astype(BF16)
    tile = 256
    tiles = cols // tile
    scale = factor * math.log2(math.e)

    def tile_cols(n):
        return pl.ds(mult(n, tile), tile)

    cuts = [0, 4, 8, 12, 15, 16] if blocks == 16 else [0, 3, 4]
    depth = 1
    for i in range(len(cuts) - 1):
        members = order[cuts[i]:cuts[i + 1]]
        while depth < max(j.bit_count() for j in members):
            depth += 1
            relay(depth)
        height = len(members) * rows
        span = pl.ds(cuts[i] * rows, height)
        for b, slot in enumerate(members):
            block = block_of(slot)
            for g in range(2):
                k_pos = group_ref[2 * block + g] * GROUP + downs
                bias[pl.ds(b * rows + g * GROUP, GROUP), :] = jnp.where(k_pos <= q_pos, 0.0, -jnp.inf)
        for b in range(latent // 128):
            turned = dot_nt(ident, kbuf[span, pl.ds(b * 128, 128)])
            lat_t[pl.ds(b * 128, 128), span] = turned.astype(BF16)

        def tile_scores(n, span=span, height=height):
            s = dot_nn(kbuf[span, :], q_t[:, n * tile:(n + 1) * tile])
            return s + jnp.concatenate([bias[0:height, :]] * (tile // 128), axis=1)

        score[0:height, 0:tile] = tile_scores(0)
        for n in range(tiles):
            tc = pl.ds(n * tile, tile)
            if n + 1 < tiles:
                score[0:height, (n + 1) * tile:(n + 2) * tile] = tile_scores(n + 1)
            gprob[span, tc] = dot_nn(kbuf[span, pl.ds(0, latent)], g_low[:, tc])
            old = peak[:, tc]
            new = jnp.maximum(old, jnp.max(score[0:height, tc], axis=0, keepdims=True))
            p = jnp.exp2((score[0:height, tc] - new) * scale)
            prob[span, tc] = p.astype(BF16)
            fade = jnp.exp2((old - new) * scale)
            total[:, tc] = total[:, tc] * fade + jnp.sum(p, axis=0, keepdims=True)
            peak[:, tc] = new
            peaks[pl.ds(i, 1), tc] = new
            o = dot_nn(lat_t[:, span], prob[span, tc])
            o_acc[:, tc] = o if i == 0 else o_acc[:, tc] * fade + o
        if i == 0:
            lax.fori_loop(0, heads // 2, project_rows, 0)
    for z in range(1, nz):
        pl.semaphore_signal(plane, inc=1, device_id=at_z(z, 0), device_id_type=MESH)
    inv[...] = 1.0 / total[...]

    def read_out(n, carry):
        tc = tile_cols(n)
        o = o_acc[:, tc] * inv[:, tc]
        o_low[:, tc] = o.astype(BF16)
        rdot[:, tc] = jnp.sum(g_t[:, tc] * o, axis=0, keepdims=True)
        return carry

    lax.fori_loop(0, tiles, read_out, 0)
    for i in range(len(cuts) - 1):
        peaks[pl.ds(i, 1), :] = jnp.exp2((peaks[pl.ds(i, 1), :] - peak[...]) * scale) * inv[...]

    core_rows = latent // 2
    hw = core_rows // 2

    def chain(w):
        first = ((nx, gx, at_x, x_offs, ny), (ny, gy, at_y, y_offs, 1))
        base = core * core_rows

        def cut(s):
            (n1, i1, a1, o1, u1), (n2, i2, a2, o2, u2) = first[s], first[1 - s]
            pairs = [(o, z) for z in range(nz) for o in range(n2) if o or z]
            return n1, i1, a1, o1, n2, i2, u2, pairs, hw // n1, hw // n1 // nz, cols // n2

        def peer(o, z, u2):
            return at_z(z, o * u2) if z else at_slot(o * u2)

        send(
            w_own.at[w, pl.ds(mult(1 - core, core_rows), core_rows)], w_core.at[w],
            wc_s.at[w], wc_r.at[w], at_core(),
        )
        yield
        arrived(w_core.at[w], wc_s.at[w], wc_r.at[w], at_core())
        mine = w_own[w, pl.ds(mult(core, core_rows), core_rows), :].astype(F32)
        w_acc[w] = (mine + w_core[w].astype(F32)).astype(BF16)
        for s in range(2):
            n1, i1, a1, o1, n2, i2, u2, pairs, r, rz, c = cut(s)
            for o in o1:
                send(
                    w_acc.at[w, pl.ds(pl.multiple_of(s * hw + flip(i1, o) * r, r), r)], w1.at[w, s, o - 1],
                    w1_s.at[w, s, o - 1], w1_r.at[w, s, o - 1], a1(o),
                )
        yield
        for s in range(2):
            n1, i1, a1, o1, n2, i2, u2, pairs, r, rz, c = cut(s)
            acc = w_acc[w, pl.ds(pl.multiple_of(s * hw + i1 * r, r), r), :].astype(F32)
            for o in o1:
                arrived(w1.at[w, s, o - 1], w1_s.at[w, s, o - 1], w1_r.at[w, s, o - 1], a1(o))
                acc = acc + w1[w, s, o - 1].astype(F32)
            w1s[w, s] = acc.astype(BF16)
            if w == 0 and s == 0 and nz > 1:
                pl.semaphore_wait(plane, nz - 1)
            for o, z in pairs:
                slot = z * n2 + o
                send(
                    w1s.at[w, s, pl.ds(mult(zs(z), rz), rz), pl.ds(mult(flip(i2, o), c), c)],
                    w2.at[w, s, slot], w2_s.at[w, s, slot], w2_r.at[w, s, slot], peer(o, z, u2),
                )
        yield

        out_ref = (val_out, key_out)[w]

        def to_core(s, o):
            n1, i1, a1, o1, n2, i2, u2, pairs, r, rz, c = cut(s)
            span = pl.ds(pl.multiple_of(base + s * hw + flip(i1, o) * r, 16), r)
            send(w_out.at[w, span], out_ref.at[span], vc_s.at[w, s, o], vc_r.at[w, s, o], at_core())

        def place(s, top, left, height, width):
            start = pl.multiple_of(base + s * hw + top, 16)
            return w_out.at[w, pl.ds(start, height), pl.ds(left, width)]

        for s in range(2):
            n1, i1, a1, o1, n2, i2, u2, pairs, r, rz, c = cut(s)
            acc = w1s[w, s, pl.ds(mult(zl, rz), rz), pl.ds(mult(i2, c), c)].astype(F32)
            for o, z in pairs:
                slot = z * n2 + o
                arrived(w2.at[w, s, slot], w2_s.at[w, s, slot], w2_r.at[w, s, slot], peer(o, z, u2))
                acc = acc + w2[w, s, slot].astype(F32)
            spot = place(s, i1 * r + zl * rz, mult(i2, c), rz, c)
            spot[...] = acc.astype(BF16)
            for o, z in pairs:
                slot = z * n2 + o
                send(spot, spot, v2_s.at[w, s, slot], v2_r.at[w, s, slot], peer(o, z, u2))
        yield
        for s in range(2):
            n1, i1, a1, o1, n2, i2, u2, pairs, r, rz, c = cut(s)
            for o, z in pairs:
                slot = z * n2 + o
                spot = place(s, i1 * r + zs(nz - z) * rz, mult(flip(i2, o), c), rz, c)
                arrived(spot, v2_s.at[w, s, slot], v2_r.at[w, s, slot], peer(o, z, u2))
            spot = place(s, i1 * r, 0, r, cols)
            for o in o1:
                send(spot, spot, v1_s.at[w, s, o - 1], v1_r.at[w, s, o - 1], a1(o))
            to_core(s, 0)
        yield
        for s in range(2):
            n1, i1, a1, o1, n2, i2, u2, pairs, r, rz, c = cut(s)
            for o in o1:
                spot = place(s, flip(i1, o) * r, 0, r, cols)
                arrived(spot, v1_s.at[w, s, o - 1], v1_r.at[w, s, o - 1], a1(o))
                to_core(s, o)
        span = pl.ds(mult(core, core_rows), core_rows)
        own = pltpu.make_async_copy(w_out.at[w, span], out_ref.at[span], out_sem.at[w])
        own.start()
        yield
        for s in range(2):
            n1, i1, a1, o1, n2, i2, u2, pairs, r, rz, c = cut(s)
            for o in [0] + o1:
                span = pl.ds(pl.multiple_of((1 - core) * core_rows + s * hw + flip(i1, o) * r, 16), r)
                arrived(out_ref.at[span], vc_s.at[w, s, o], vc_r.at[w, s, o], at_core())
        own.wait()
        yield

    def value_head(h):
        hc = pl.ds(h * 128, 128)
        w_own[0, :, hc] = dot_nn(o_low[:, hc], go[:, hc]).astype(BF16)

    def grade(n):
        tc = pl.ds(n * tile, tile)
        for i in range(len(cuts) - 1):
            for j in range(cuts[i], cuts[i + 1]):
                span = pl.ds(j * rows, rows)
                p = prob[span, tc].astype(F32) * peaks[pl.ds(i, 1), tc]
                prob[span, tc] = p.astype(BF16)
                dscore[span, tc] = (p * (gprob[span, tc] - rdot[:, tc])).astype(BF16)

    def query_grad(n):
        tc = pl.ds(n * tile, tile)
        gq_low[:, tc] = (dot_nn(lat_t[...], dscore[:, tc]) * factor).astype(BF16)

    def key_head(h):
        hc = pl.ds(h * 128, 128)
        w_own[1, :, hc] = dot_nn(gq_low[:, hc], qn[:, hc]).astype(BF16)

    if bits == 4:
        stages = (((0,), (1,), (2, 3)), ((2,), (3,), (0, 1)), ((1,), (0,), (2, 3)), ((3,), (2,), (0, 1)))
    else:
        stages = (((0,), (1,)), ((1,), (0,)), ((0,), (1,)), ((1,), (0,)))
    width = latent // 4
    round_of = {slot: chunks - 1 - place_of[slot] // 4 for slot in range(blocks)}

    def masks(k):
        return [sum(1 << t for t in group) for group in stages[k]]

    def stage_of(k, slot):
        return next((t for t, m in enumerate(masks(k)) if slot & m), len(stages[k]))

    def sources(k, slot):
        return [
            (slot | h, h) for m in masks(k)[:stage_of(k, slot)] for h in range(1, blocks) if h & m == h
        ]

    def ready(k, slot):
        return max([round_of[slot]] + [ready(k, src) + 1 for src, _ in sources(k, slot)])

    def latent_piece(k, slot):
        return lsend.at[pl.ds(place_of[slot] * rows, rows), pl.ds(k * width, width)]

    def latent_sum(k, slot):
        acc = latent_piece(k, slot)[...].astype(F32)
        for src, hop in sources(k, slot):
            arrived(lrecv.at[k, src], l_s.at[k, src], l_r.at[k, src], at_slot(hop))
            acc = acc + lrecv[k, src].astype(F32)
        return acc

    def latent_send(k, slot):
        if sources(k, slot):
            latent_piece(k, slot)[...] = latent_sum(k, slot).astype(BF16)
        hop = slot & masks(k)[stage_of(k, slot)]
        send(latent_piece(k, slot), lrecv.at[k, slot], l_s.at[k, slot], l_r.at[k, slot], at_slot(hop))

    def latent_chunk(n):
        span = pl.ds((chunks - 1 - n) * chunk, chunk)
        for c in range(2):
            cs = pl.ds(c * half_lat, half_lat)
            part_sum = dot_nn(prob[span, :], g_nat[:, cs]) + dot_nn(dscore[span, :], q_nat[:, cs])
            lsend[span, cs] = part_sum.astype(BF16)

    def latent_sends(n):
        todo = [
            (stage_of(k, j), -place_of[j], k, j)
            for j in range(1, blocks) for k in range(4) if min(ready(k, j), chunks - 1) == n
        ]
        for _, _, k, j in sorted(todo):
            latent_send(k, j)

    share = latent // nh
    chains = {"v": chain(0), "k": chain(1)}

    def latent_heads():
        for k in range(4):
            lzs[:, pl.ds(k * width, width)] = latent_sum(k, 0).astype(BF16)
        for o in range(1, nh):
            send(
                lzs.at[:, pl.ds(mult(lax.rem(head + o, nh), share), share)], lzr.at[o - 1],
                lz_s.at[o - 1], lz_r.at[o - 1], at_head(o),
            )

    def latent_finish():
        acc = lzs[:, pl.ds(mult(head, share), share)].astype(F32)
        for o in range(1, nh):
            arrived(lzr.at[o - 1], lz_s.at[o - 1], lz_r.at[o - 1], at_head(o))
            acc = acc + lzr[o - 1].astype(F32)
        lat_v[...] = acc.astype(BF16)
        last = pltpu.make_async_copy(lat_v, lat_out, out_sem.at[2])
        last.start()
        last.wait()

    for op in PLAN:
        if op in chains:
            next(chains[op])
        elif op == "value":
            for h in range(heads):
                value_head(h)
        elif op == "query":
            for n in range(tiles):
                grade(n)
                query_grad(n)
        elif op == "key":
            for h in range(heads):
                key_head(h)
        elif op == "heads":
            latent_heads()
        elif op == "finish":
            latent_finish()
        elif int(op[1]) < chunks:
            (latent_chunk if op[0] == "c" else latent_sends)(int(op[1]))
    for copy in sends:
        copy.wait_send()


def widen(lat_ref, key_ref, value_ref, lat_out, key_out, value_out, lat_v, low, wide, in_sem, out_sem):
    tall = low.shape[1] // CUTS
    pairs = ((key_ref, key_out), (value_ref, value_out))
    loads, stores = [], []
    for c in range(CUTS):
        for a, (src, _) in enumerate(pairs):
            span = pl.ds(c * tall, tall)
            loads.append(pltpu.make_async_copy(src.at[span], low.at[a, span], in_sem.at[a, c]))
            loads[-1].start()
    lat = pltpu.make_async_copy(lat_ref, lat_v, in_sem.at[2, 0])
    lat.start()
    for c in range(CUTS):
        for a, (_, dst) in enumerate(pairs):
            span = pl.ds(c * tall, tall)
            loads[2 * c + a].wait()
            wide[a, span, :] = low[a, span, :].astype(F32)
            stores.append(pltpu.make_async_copy(wide.at[a, span], dst.at[span], out_sem.at[a, c]))
            stores[-1].start()
    lat.wait()
    stores.append(pltpu.make_async_copy(lat_v, lat_out, out_sem.at[2, 0]))
    stores[-1].start()
    for copy in stores:
        copy.wait()


def shards(query_nope, query_rope, latent, rope_key, key_up, value_up, grad_out, group_order):
    ctx, nh, dp = (lax.axis_size(a) for a in ("ctx", "head", "dp"))
    nx = math.isqrt(ctx)
    ny = ctx // nx
    nz = dp // 2
    rows = query_nope.shape[1]
    cols = key_up.shape[1]
    heads = cols // HEAD_DIM
    rope = rope_key.shape[2]
    width = latent.shape[2]
    keys = ctx * rows
    bits = ctx.bit_length() - 1
    hw = width // 4
    r1 = hw // nx
    share = width // nh
    factor = 1.0 / math.sqrt(HEAD_DIM + rope)
    dims = (nx, ny, nh, nz, heads, width, rope, factor)
    vmem = pltpu.VMEM
    dma = pltpu.SemaphoreType.DMA
    n3 = max(nx - 1, 1)
    h3 = max(nh - 1, 1)
    scratch = [
        vmem((keys, width + 128), BF16),
        vmem((width, keys), BF16),
        vmem((rows, cols), BF16),
        vmem((rows, heads * rope), BF16),
        vmem((width, cols), BF16),
        vmem((width, cols), BF16),
        vmem((rows, cols), BF16),
        vmem((rope, rows), BF16),
        vmem((width + 128, cols), BF16),
        vmem((width, cols), F32),
        vmem((width, cols), BF16),
        vmem((512, cols), F32),
        vmem((keys, cols), F32),
        vmem((keys, cols), BF16),
        vmem((keys, cols), BF16),
        vmem((512, 128), F32),
        vmem((1, cols), F32),
        vmem((8, cols), F32),
        vmem((1, cols), F32),
        vmem((1, cols), F32),
        vmem((1, cols), F32),
        vmem((width, cols), F32),
        vmem((width, cols), BF16),
        vmem((width, cols), BF16),
        vmem((cols, width), BF16),
        vmem((cols, width), BF16),
        vmem((keys, width), BF16),
        vmem((4, ctx, rows, width // 4), BF16),
        vmem((rows, width), BF16),
        vmem((h3, rows, share), BF16),
        vmem((rows, share), BF16),
        vmem((2, width, cols), BF16),
        vmem((2, width // 2, cols), BF16),
        vmem((2, width // 2, cols), BF16),
        vmem((2, 2, n3, r1, cols), BF16),
        vmem((2, 2, r1, cols), BF16),
        vmem((2, 2, ny * nz, r1 // nz, cols // ny), BF16),
        vmem((2, width, cols), BF16),
        dma((7,)), dma((3,)),
        dma((bits, ctx)), dma((bits, ctx)),
        dma((4, ctx)), dma((4, ctx)),
        dma((h3,)), dma((h3,)),
        dma((2,)), dma((2,)),
        dma((2, 2, n3)), dma((2, 2, n3)),
        dma((2, 2, ny * nz)), dma((2, 2, ny * nz)),
        dma((2, 2, ny * nz)), dma((2, 2, ny * nz)),
        dma((2, 2, n3)), dma((2, 2, n3)),
        dma((2, 2, nx)), dma((2, 2, nx)),
        pltpu.SemaphoreType.REGULAR,
    ]
    hbm = pl.BlockSpec(memory_space=pl.ANY)
    lat, key_grad, value_grad = pl.pallas_call(
        functools.partial(kernel, dims),
        out_shape=(
            jax.ShapeDtypeStruct((rows, share), BF16),
            jax.ShapeDtypeStruct((width, cols), BF16),
            jax.ShapeDtypeStruct((width, cols), BF16),
        ),
        in_specs=[pl.BlockSpec(memory_space=pltpu.SMEM)] + [hbm] * 7,
        out_specs=(hbm, hbm, hbm),
        scratch_shapes=scratch,
        compiler_params=pltpu.CompilerParams(
            collective_id=0, has_side_effects=True, vmem_limit_bytes=60 * 1024 * 1024
        ),
        cost_estimate=pl.CostEstimate(flops=15_000_000_000, bytes_accessed=8_000_000, transcendentals=2_000_000),
    )(
        group_order, latent[0], rope_key[0].T, query_nope[0], query_rope[0],
        key_up, value_up, grad_out[0],
    )
    lat, key_grad, value_grad = pl.pallas_call(
        widen,
        out_shape=(
            jax.ShapeDtypeStruct((rows, share), BF16),
            jax.ShapeDtypeStruct((width, cols), F32),
            jax.ShapeDtypeStruct((width, cols), F32),
        ),
        in_specs=[hbm] * 3,
        out_specs=(hbm,) * 3,
        scratch_shapes=[
            vmem((rows, share), BF16), vmem((2, width, cols), BF16), vmem((2, width, cols), F32),
            dma((3, CUTS)), dma((3, CUTS)),
        ],
        compiler_params=pltpu.CompilerParams(vmem_limit_bytes=60 * 1024 * 1024),
    )(lat, key_grad, value_grad)
    return lat[None], key_grad, value_grad


def solution(mesh):
    in_specs = (
        P("dp", "ctx", "head"),
        P("dp", "ctx", "head"),
        P("dp", "ctx", None),
        P("dp", "ctx", None),
        P(None, "head"),
        P(None, "head"),
        P("dp", "ctx", "head"),
        P(),
    )
    out_specs = (P("dp", "ctx", "head"), P(None, "head"), P(None, "head"))
    return jax.shard_map(shards, mesh=mesh, in_specs=in_specs, out_specs=out_specs, check_vma=False)
```

```python
import functools
import math

import jax
import jax.numpy as jnp
from jax import lax
from jax.experimental import pallas as pl
from jax.experimental.pallas import tpu as pltpu
from jax.sharding import PartitionSpec as P

HEAD_DIM = 128
GROUP = 64
F32 = jnp.float32
BF16 = jnp.bfloat16
MESH = pl.DeviceIdType.MESH
CUTS = 4
PLAN = ("value", "v", "query", "v", "key", "k", "c0", "k", "v", "c1", "s0", "c2", "k", "v", "s1", "c3", "s2", "k", "v", "s3", "k", "v", "heads", "k", "finish", "v", "k")


def dot_nn(left, right):
    return lax.dot_general(left, right, (((1,), (0,)), ((), ())), preferred_element_type=F32)


def dot_nt(left, right):
    return lax.dot_general(left, right, (((1,), (1,)), ((), ())), preferred_element_type=F32)


def dot_tn(left, right):
    return lax.dot_general(left, right, (((0,), (0,)), ((), ())), preferred_element_type=F32)


def mult(value, factor):
    return pl.multiple_of(value * factor, factor)


def kernel(dims, *refs):
    (nx, ny, nh, nz, heads, latent, rope, factor) = dims
    (
        group_ref, lat_ref, rk_ref, qn_ref, qr_ref, ku_ref, vu_ref, go_ref,
        lat_out, key_out, val_out,
        kbuf, lat_t, qn, qr, ku, vu, go, rk,
        q_t, g_t, g_low, score, gprob, prob, dscore,
        bias, peak, peaks, total, inv, rdot,
        o_acc, o_low, gq_low, g_nat, q_nat,
        lsend, lrecv, lzs, lzr, lat_v,
        w_own, w_core, w_acc, w1, w1s, w2, w_out,
        in_sem, out_sem, ag_s, ag_r, l_s, l_r, lz_s, lz_r,
        wc_s, wc_r, w1_s, w1_r, w2_s, w2_r,
        v2_s, v2_r, v1_s, v1_r, vc_s, vc_r, plane,
    ) = refs
    rows = 128
    blocks = nx * ny
    keys = blocks * rows
    cols = heads * HEAD_DIM
    half_lat = latent // 2
    bits = blocks.bit_length() - 1
    chunk = 4 * rows
    chunks = blocks // 4

    ctx = lax.axis_index("ctx")
    head = lax.axis_index("head")
    dp = lax.axis_index("dp")
    zl, core = dp // 2, lax.rem(dp, 2)

    def gray(v):
        return v // 2 * 2 + lax.rem(v // 2 + lax.rem(v, 2), 2)

    def flip(v, off):
        return lax.rem(v // 2 + off // 2, 2) * 2 + lax.rem(lax.rem(v, 2) + off % 2, 2)

    gx, gy = gray(ctx // ny), gray(lax.rem(ctx, ny))

    def block_of(slot):
        return gray(flip(gx, slot // ny)) * ny + gray(flip(gy, slot % ny))

    def at_slot(slot):
        return {"ctx": block_of(slot)}

    def at_x(off):
        return at_slot(off * ny)

    def at_y(off):
        return at_slot(off)

    def at_core():
        return {"dp": zl * 2 + 1 - core}

    def zs(off):
        return lax.rem(zl + off, nz)

    def at_z(off, slot):
        where = {"dp": zs(off) * 2 + core}
        return {**at_slot(slot), **where} if slot else where

    def at_head(off):
        return {"head": lax.rem(head + off, nh)}

    x_offs = sorted(range(1, nx), key=lambda o: -o.bit_count())
    y_offs = sorted(range(1, ny), key=lambda o: -o.bit_count())
    partners = (
        [at_slot(1 << t) for t in range(bits)] + [at_core()]
        + [at_z(z, 0) for z in range(1, nz)] + [at_head(o) for o in range(1, nh)]
    )
    order = sorted(range(blocks), key=lambda j: (j.bit_count(), j))
    place_of = {j: i for i, j in enumerate(order)}

    sends = []

    def send(src, dst, ssem, rsem, where):
        copy = pltpu.make_async_remote_copy(
            src_ref=src, dst_ref=dst, send_sem=ssem, recv_sem=rsem,
            device_id=where, device_id_type=MESH,
        )
        copy.start()
        sends.append(copy)

    def arrived(dst, ssem, rsem, where):
        pltpu.make_async_remote_copy(
            src_ref=dst, dst_ref=dst, send_sem=ssem, recv_sem=rsem,
            device_id=where, device_id_type=MESH,
        ).wait_recv()

    barrier = pltpu.get_barrier_semaphore()
    for where in partners:
        pl.semaphore_signal(barrier, inc=1, device_id=where, device_id_type=MESH)

    own_rows = pl.ds(0, rows)
    loads = [
        pltpu.make_async_copy(lat_ref, kbuf.at[own_rows, pl.ds(0, latent)], in_sem.at[0]),
        pltpu.make_async_copy(rk_ref, rk, in_sem.at[1]),
        pltpu.make_async_copy(qn_ref, qn, in_sem.at[2]),
        pltpu.make_async_copy(ku_ref, ku, in_sem.at[3]),
        pltpu.make_async_copy(qr_ref, qr, in_sem.at[4]),
        pltpu.make_async_copy(go_ref, go, in_sem.at[5]),
        pltpu.make_async_copy(vu_ref, vu, in_sem.at[6]),
    ]
    for copy in loads:
        copy.start()

    loads[1].wait()
    spread = lax.broadcasted_iota(jnp.int32, (rope, 128), 0)
    lane = lax.broadcasted_iota(jnp.int32, (rope, 128), 1)
    twice = jnp.where(spread == lax.rem(lane, rope), 1.0, 0.0).astype(BF16)
    kbuf[own_rows, pl.ds(latent, 128)] = dot_tn(rk[...], twice).astype(BF16)
    loads[0].wait()
    pl.semaphore_wait(barrier, len(partners))

    part = rows // bits

    def piece(k, slot):
        return kbuf.at[pl.ds(place_of[slot] * rows + k * part, part)]

    def gather_send(k, slot, step):
        bit = 1 << ((k + step) % bits)
        there = slot ^ bit
        send(piece(k, slot), piece(k, there), ag_s.at[k, there], ag_r.at[k, there], at_slot(bit))

    def last_step(k, slot):
        return max([-1] + [t for t in range(bits) if slot >> ((k + t) % bits) & 1])

    def relay(depth):
        todo = [(last_step(k, j), j, k) for k in range(bits) for j in range(blocks) if j.bit_count() == depth]
        for last, slot, k in sorted(todo):
            arrived(piece(k, slot), ag_s.at[k, slot], ag_r.at[k, slot], at_slot(1))
            for step in range(last + 1, bits):
                gather_send(k, slot, step)

    for step in range(bits):
        for k in range(bits):
            gather_send(k, 0, step)

    for copy in loads[2:]:
        copy.wait()
    row_id = lax.broadcasted_iota(jnp.int32, (128, 128), 0)
    col_id = lax.broadcasted_iota(jnp.int32, (128, 128), 1)
    eye = row_id == col_id

    def head_cols(h):
        return pl.ds(mult(h, 128), 128)

    def project(i, carry):
        for h in (2 * i, 2 * i + 1):
            hc = head_cols(h)
            q_t[pl.ds(0, latent), hc] = dot_nt(ku[:, hc], qn[:, hc]).astype(BF16)
            pick = jnp.where(eye & (row_id // rope == lax.rem(h, 2)), 1.0, 0.0).astype(BF16)
            pair = qr[:, pl.ds(mult(i, 128), 128)]
            q_t[pl.ds(latent, 128), hc] = dot_nt(pick, pair).astype(BF16)
            grad = dot_nt(vu[:, hc], go[:, hc])
            g_t[:, hc] = grad
            g_low[:, hc] = grad.astype(BF16)
        return carry

    lax.fori_loop(0, heads // 2, project, 0)
    relay(1)

    def project_rows(i, carry):
        for h in (2 * i, 2 * i + 1):
            hc = head_cols(h)
            g_nat[hc, :] = dot_nt(go[:, hc], vu[:, hc]).astype(BF16)
            q_nat[hc, :] = (dot_nt(qn[:, hc], ku[:, hc]) * factor).astype(BF16)
        return carry

    lanes = lax.broadcasted_iota(jnp.int32, (GROUP, 128), 1)
    downs = lax.broadcasted_iota(jnp.int32, (GROUP, 128), 0)
    own_low, own_high = group_ref[2 * ctx], group_ref[2 * ctx + 1]
    q_pos = jnp.where(lanes < GROUP, own_low * GROUP + lanes, own_high * GROUP + lanes - GROUP)
    peak[...] = jnp.full(peak.shape, -1e30, F32)
    total[...] = jnp.zeros(total.shape, F32)
    ident = jnp.where(eye, 1.0, 0.0).astype(BF16)
    tile = 256
    tiles = cols // tile
    scale = factor * math.log2(math.e)

    def tile_cols(n):
        return pl.ds(mult(n, tile), tile)

    cuts = [0, 4, 8, 12, 15, 16] if blocks == 16 else [0, 3, 4]
    depth = 1
    for i in range(len(cuts) - 1):
        members = order[cuts[i]:cuts[i + 1]]
        while depth < max(j.bit_count() for j in members):
            depth += 1
            relay(depth)
        height = len(members) * rows
        span = pl.ds(cuts[i] * rows, height)
        for b, slot in enumerate(members):
            block = block_of(slot)
            for g in range(2):
                k_pos = group_ref[2 * block + g] * GROUP + downs
                bias[pl.ds(b * rows + g * GROUP, GROUP), :] = jnp.where(k_pos <= q_pos, 0.0, -jnp.inf)
        for b in range(latent // 128):
            turned = dot_nt(ident, kbuf[span, pl.ds(b * 128, 128)])
            lat_t[pl.ds(b * 128, 128), span] = turned.astype(BF16)

        def tile_scores(n, span=span, height=height):
            s = dot_nn(kbuf[span, :], q_t[:, n * tile:(n + 1) * tile])
            return s + jnp.concatenate([bias[0:height, :]] * (tile // 128), axis=1)

        score[0:height, 0:tile] = tile_scores(0)
        for n in range(tiles):
            tc = pl.ds(n * tile, tile)
            if n + 1 < tiles:
                score[0:height, (n + 1) * tile:(n + 2) * tile] = tile_scores(n + 1)
            gprob[span, tc] = dot_nn(kbuf[span, pl.ds(0, latent)], g_low[:, tc])
            old = peak[:, tc]
            new = jnp.maximum(old, jnp.max(score[0:height, tc], axis=0, keepdims=True))
            p = jnp.exp2((score[0:height, tc] - new) * scale)
            prob[span, tc] = p.astype(BF16)
            fade = jnp.exp2((old - new) * scale)
            total[:, tc] = total[:, tc] * fade + jnp.sum(p, axis=0, keepdims=True)
            peak[:, tc] = new
            peaks[pl.ds(i, 1), tc] = new
            o = dot_nn(lat_t[:, span], prob[span, tc])
            o_acc[:, tc] = o if i == 0 else o_acc[:, tc] * fade + o
        if i == 0:
            lax.fori_loop(0, heads // 2, project_rows, 0)
    for z in range(1, nz):
        pl.semaphore_signal(plane, inc=1, device_id=at_z(z, 0), device_id_type=MESH)
    inv[...] = 1.0 / total[...]

    def read_out(n, carry):
        tc = tile_cols(n)
        o = o_acc[:, tc] * inv[:, tc]
        o_low[:, tc] = o.astype(BF16)
        rdot[:, tc] = jnp.sum(g_t[:, tc] * o, axis=0, keepdims=True)
        return carry

    lax.fori_loop(0, tiles, read_out, 0)
    for i in range(len(cuts) - 1):
        peaks[pl.ds(i, 1), :] = jnp.exp2((peaks[pl.ds(i, 1), :] - peak[...]) * scale) * inv[...]

    core_rows = latent // 2
    hw = core_rows // 2

    def chain(w):
        first = ((nx, gx, at_x, x_offs, ny), (ny, gy, at_y, y_offs, 1))
        base = core * core_rows

        def cut(s):
            (n1, i1, a1, o1, u1), (n2, i2, a2, o2, u2) = first[s], first[1 - s]
            pairs = [(o, z) for z in range(nz) for o in range(n2) if o or z]
            pairs.sort(key=lambda p: -p[0].bit_count() - p[1])
            return n1, i1, a1, o1, n2, i2, u2, pairs, hw // n1, hw // n1 // nz, cols // n2

        def peer(o, z, u2):
            return at_z(z, o * u2) if z else at_slot(o * u2)

        send(
            w_own.at[w, pl.ds(mult(1 - core, core_rows), core_rows)], w_core.at[w],
            wc_s.at[w], wc_r.at[w], at_core(),
        )
        yield
        arrived(w_core.at[w], wc_s.at[w], wc_r.at[w], at_core())
        mine = w_own[w, pl.ds(mult(core, core_rows), core_rows), :].astype(F32)
        w_acc[w] = (mine + w_core[w].astype(F32)).astype(BF16)
        for s in range(2):
            n1, i1, a1, o1, n2, i2, u2, pairs, r, rz, c = cut(s)
            for o in o1:
                send(
                    w_acc.at[w, pl.ds(pl.multiple_of(s * hw + flip(i1, o) * r, r), r)], w1.at[w, s, o - 1],
                    w1_s.at[w, s, o - 1], w1_r.at[w, s, o - 1], a1(o),
                )
        yield
        for s in range(2):
            n1, i1, a1, o1, n2, i2, u2, pairs, r, rz, c = cut(s)
            acc = w_acc[w, pl.ds(pl.multiple_of(s * hw + i1 * r, r), r), :].astype(F32)
            for o in o1:
                arrived(w1.at[w, s, o - 1], w1_s.at[w, s, o - 1], w1_r.at[w, s, o - 1], a1(o))
                acc = acc + w1[w, s, o - 1].astype(F32)
            w1s[w, s] = acc.astype(BF16)
            if w == 0 and s == 0 and nz > 1:
                pl.semaphore_wait(plane, nz - 1)
            for o, z in pairs:
                slot = z * n2 + o
                send(
                    w1s.at[w, s, pl.ds(mult(zs(z), rz), rz), pl.ds(mult(flip(i2, o), c), c)],
                    w2.at[w, s, slot], w2_s.at[w, s, slot], w2_r.at[w, s, slot], peer(o, z, u2),
                )
        yield

        out_ref = (val_out, key_out)[w]

        def to_core(s, o):
            n1, i1, a1, o1, n2, i2, u2, pairs, r, rz, c = cut(s)
            span = pl.ds(pl.multiple_of(base + s * hw + flip(i1, o) * r, 16), r)
            send(w_out.at[w, span], out_ref.at[span], vc_s.at[w, s, o], vc_r.at[w, s, o], at_core())

        def place(s, top, left, height, width):
            start = pl.multiple_of(base + s * hw + top, 16)
            return w_out.at[w, pl.ds(start, height), pl.ds(left, width)]

        for s in range(2):
            n1, i1, a1, o1, n2, i2, u2, pairs, r, rz, c = cut(s)
            acc = w1s[w, s, pl.ds(mult(zl, rz), rz), pl.ds(mult(i2, c), c)].astype(F32)
            for o, z in pairs:
                slot = z * n2 + o
                arrived(w2.at[w, s, slot], w2_s.at[w, s, slot], w2_r.at[w, s, slot], peer(o, z, u2))
                acc = acc + w2[w, s, slot].astype(F32)
            spot = place(s, i1 * r + zl * rz, mult(i2, c), rz, c)
            spot[...] = acc.astype(BF16)
            for o, z in pairs:
                slot = z * n2 + o
                send(spot, spot, v2_s.at[w, s, slot], v2_r.at[w, s, slot], peer(o, z, u2))
        yield
        for s in range(2):
            n1, i1, a1, o1, n2, i2, u2, pairs, r, rz, c = cut(s)
            for o, z in pairs:
                slot = z * n2 + o
                spot = place(s, i1 * r + zs(nz - z) * rz, mult(flip(i2, o), c), rz, c)
                arrived(spot, v2_s.at[w, s, slot], v2_r.at[w, s, slot], peer(o, z, u2))
            spot = place(s, i1 * r, 0, r, cols)
            for o in o1:
                send(spot, spot, v1_s.at[w, s, o - 1], v1_r.at[w, s, o - 1], a1(o))
            to_core(s, 0)
        yield
        for s in range(2):
            n1, i1, a1, o1, n2, i2, u2, pairs, r, rz, c = cut(s)
            for o in o1:
                spot = place(s, flip(i1, o) * r, 0, r, cols)
                arrived(spot, v1_s.at[w, s, o - 1], v1_r.at[w, s, o - 1], a1(o))
                to_core(s, o)
        span = pl.ds(mult(core, core_rows), core_rows)
        own = pltpu.make_async_copy(w_out.at[w, span], out_ref.at[span], out_sem.at[w])
        own.start()
        yield
        for s in range(2):
            n1, i1, a1, o1, n2, i2, u2, pairs, r, rz, c = cut(s)
            for o in [0] + o1:
                span = pl.ds(pl.multiple_of((1 - core) * core_rows + s * hw + flip(i1, o) * r, 16), r)
                arrived(out_ref.at[span], vc_s.at[w, s, o], vc_r.at[w, s, o], at_core())
        own.wait()
        yield

    def value_head(h):
        hc = pl.ds(h * 128, 128)
        w_own[0, :, hc] = dot_nn(o_low[:, hc], go[:, hc]).astype(BF16)

    def grade(n):
        tc = pl.ds(n * tile, tile)
        for i in range(len(cuts) - 1):
            for j in range(cuts[i], cuts[i + 1]):
                span = pl.ds(j * rows, rows)
                p = prob[span, tc].astype(F32) * peaks[pl.ds(i, 1), tc]
                prob[span, tc] = p.astype(BF16)
                dscore[span, tc] = (p * (gprob[span, tc] - rdot[:, tc])).astype(BF16)

    def query_grad(n):
        tc = pl.ds(n * tile, tile)
        gq_low[:, tc] = (dot_nn(lat_t[...], dscore[:, tc]) * factor).astype(BF16)

    def key_head(h):
        hc = pl.ds(h * 128, 128)
        w_own[1, :, hc] = dot_nn(gq_low[:, hc], qn[:, hc]).astype(BF16)

    if bits == 4:
        stages = (((0,), (1,), (2, 3)), ((2,), (3,), (0, 1)), ((1,), (0,), (2, 3)), ((3,), (2,), (0, 1)))
    else:
        stages = (((0,), (1,)), ((1,), (0,)), ((0,), (1,)), ((1,), (0,)))
    width = latent // 4
    round_of = {slot: chunks - 1 - place_of[slot] // 4 for slot in range(blocks)}

    def masks(k):
        return [sum(1 << t for t in group) for group in stages[k]]

    def stage_of(k, slot):
        return next((t for t, m in enumerate(masks(k)) if slot & m), len(stages[k]))

    def sources(k, slot):
        return [
            (slot | h, h) for m in masks(k)[:stage_of(k, slot)] for h in range(1, blocks) if h & m == h
        ]

    def ready(k, slot):
        return max([round_of[slot]] + [ready(k, src) + 1 for src, _ in sources(k, slot)])

    def latent_piece(k, slot):
        return lsend.at[pl.ds(place_of[slot] * rows, rows), pl.ds(k * width, width)]

    def latent_sum(k, slot):
        acc = latent_piece(k, slot)[...].astype(F32)
        for src, hop in sources(k, slot):
            arrived(lrecv.at[k, src], l_s.at[k, src], l_r.at[k, src], at_slot(hop))
            acc = acc + lrecv[k, src].astype(F32)
        return acc

    def latent_send(k, slot):
        if sources(k, slot):
            latent_piece(k, slot)[...] = latent_sum(k, slot).astype(BF16)
        hop = slot & masks(k)[stage_of(k, slot)]
        send(latent_piece(k, slot), lrecv.at[k, slot], l_s.at[k, slot], l_r.at[k, slot], at_slot(hop))

    def latent_chunk(n):
        span = pl.ds((chunks - 1 - n) * chunk, chunk)
        for c in range(2):
            cs = pl.ds(c * half_lat, half_lat)
            part_sum = dot_nn(prob[span, :], g_nat[:, cs]) + dot_nn(dscore[span, :], q_nat[:, cs])
            lsend[span, cs] = part_sum.astype(BF16)

    def latent_sends(n):
        todo = [
            (stage_of(k, j), -place_of[j], k, j)
            for j in range(1, blocks) for k in range(4) if min(ready(k, j), chunks - 1) == n
        ]
        for _, _, k, j in sorted(todo):
            latent_send(k, j)

    share = latent // nh
    chains = {"v": chain(0), "k": chain(1)}

    def latent_heads():
        for k in range(4):
            lzs[:, pl.ds(k * width, width)] = latent_sum(k, 0).astype(BF16)
        for o in range(1, nh):
            send(
                lzs.at[:, pl.ds(mult(lax.rem(head + o, nh), share), share)], lzr.at[o - 1],
                lz_s.at[o - 1], lz_r.at[o - 1], at_head(o),
            )

    def latent_finish():
        acc = lzs[:, pl.ds(mult(head, share), share)].astype(F32)
        for o in range(1, nh):
            arrived(lzr.at[o - 1], lz_s.at[o - 1], lz_r.at[o - 1], at_head(o))
            acc = acc + lzr[o - 1].astype(F32)
        lat_v[...] = acc.astype(BF16)
        last = pltpu.make_async_copy(lat_v, lat_out, out_sem.at[2])
        last.start()
        last.wait()

    for op in PLAN:
        if op in chains:
            next(chains[op])
        elif op == "value":
            for h in range(heads):
                value_head(h)
        elif op == "query":
            for n in range(tiles):
                grade(n)
                query_grad(n)
        elif op == "key":
            for h in range(heads):
                key_head(h)
        elif op == "heads":
            latent_heads()
        elif op == "finish":
            latent_finish()
        elif int(op[1]) < chunks:
            (latent_chunk if op[0] == "c" else latent_sends)(int(op[1]))
    for copy in sends:
        copy.wait_send()


def widen(lat_ref, key_ref, value_ref, lat_out, key_out, value_out, lat_v, low, wide, in_sem, out_sem):
    tall = low.shape[1] // CUTS
    pairs = ((key_ref, key_out), (value_ref, value_out))
    loads, stores = [], []
    for c in range(CUTS):
        for a, (src, _) in enumerate(pairs):
            span = pl.ds(c * tall, tall)
            loads.append(pltpu.make_async_copy(src.at[span], low.at[a, span], in_sem.at[a, c]))
            loads[-1].start()
    lat = pltpu.make_async_copy(lat_ref, lat_v, in_sem.at[2, 0])
    lat.start()
    for c in range(CUTS):
        for a, (_, dst) in enumerate(pairs):
            span = pl.ds(c * tall, tall)
            loads[2 * c + a].wait()
            wide[a, span, :] = low[a, span, :].astype(F32)
            stores.append(pltpu.make_async_copy(wide.at[a, span], dst.at[span], out_sem.at[a, c]))
            stores[-1].start()
    lat.wait()
    stores.append(pltpu.make_async_copy(lat_v, lat_out, out_sem.at[2, 0]))
    stores[-1].start()
    for copy in stores:
        copy.wait()


def shards(query_nope, query_rope, latent, rope_key, key_up, value_up, grad_out, group_order):
    ctx, nh, dp = (lax.axis_size(a) for a in ("ctx", "head", "dp"))
    nx = math.isqrt(ctx)
    ny = ctx // nx
    nz = dp // 2
    rows = query_nope.shape[1]
    cols = key_up.shape[1]
    heads = cols // HEAD_DIM
    rope = rope_key.shape[2]
    width = latent.shape[2]
    keys = ctx * rows
    bits = ctx.bit_length() - 1
    hw = width // 4
    r1 = hw // nx
    share = width // nh
    factor = 1.0 / math.sqrt(HEAD_DIM + rope)
    dims = (nx, ny, nh, nz, heads, width, rope, factor)
    vmem = pltpu.VMEM
    dma = pltpu.SemaphoreType.DMA
    n3 = max(nx - 1, 1)
    h3 = max(nh - 1, 1)
    scratch = [
        vmem((keys, width + 128), BF16),
        vmem((width, keys), BF16),
        vmem((rows, cols), BF16),
        vmem((rows, heads * rope), BF16),
        vmem((width, cols), BF16),
        vmem((width, cols), BF16),
        vmem((rows, cols), BF16),
        vmem((rope, rows), BF16),
        vmem((width + 128, cols), BF16),
        vmem((width, cols), F32),
        vmem((width, cols), BF16),
        vmem((512, cols), F32),
        vmem((keys, cols), F32),
        vmem((keys, cols), BF16),
        vmem((keys, cols), BF16),
        vmem((512, 128), F32),
        vmem((1, cols), F32),
        vmem((8, cols), F32),
        vmem((1, cols), F32),
        vmem((1, cols), F32),
        vmem((1, cols), F32),
        vmem((width, cols), F32),
        vmem((width, cols), BF16),
        vmem((width, cols), BF16),
        vmem((cols, width), BF16),
        vmem((cols, width), BF16),
        vmem((keys, width), BF16),
        vmem((4, ctx, rows, width // 4), BF16),
        vmem((rows, width), BF16),
        vmem((h3, rows, share), BF16),
        vmem((rows, share), BF16),
        vmem((2, width, cols), BF16),
        vmem((2, width // 2, cols), BF16),
        vmem((2, width // 2, cols), BF16),
        vmem((2, 2, n3, r1, cols), BF16),
        vmem((2, 2, r1, cols), BF16),
        vmem((2, 2, ny * nz, r1 // nz, cols // ny), BF16),
        vmem((2, width, cols), BF16),
        dma((7,)), dma((3,)),
        dma((bits, ctx)), dma((bits, ctx)),
        dma((4, ctx)), dma((4, ctx)),
        dma((h3,)), dma((h3,)),
        dma((2,)), dma((2,)),
        dma((2, 2, n3)), dma((2, 2, n3)),
        dma((2, 2, ny * nz)), dma((2, 2, ny * nz)),
        dma((2, 2, ny * nz)), dma((2, 2, ny * nz)),
        dma((2, 2, n3)), dma((2, 2, n3)),
        dma((2, 2, nx)), dma((2, 2, nx)),
        pltpu.SemaphoreType.REGULAR,
    ]
    hbm = pl.BlockSpec(memory_space=pl.ANY)
    lat, key_grad, value_grad = pl.pallas_call(
        functools.partial(kernel, dims),
        out_shape=(
            jax.ShapeDtypeStruct((rows, share), BF16),
            jax.ShapeDtypeStruct((width, cols), BF16),
            jax.ShapeDtypeStruct((width, cols), BF16),
        ),
        in_specs=[pl.BlockSpec(memory_space=pltpu.SMEM)] + [hbm] * 7,
        out_specs=(hbm, hbm, hbm),
        scratch_shapes=scratch,
        compiler_params=pltpu.CompilerParams(
            collective_id=0, has_side_effects=True, vmem_limit_bytes=60 * 1024 * 1024
        ),
        cost_estimate=pl.CostEstimate(flops=15_000_000_000, bytes_accessed=8_000_000, transcendentals=2_000_000),
    )(
        group_order, latent[0], rope_key[0].T, query_nope[0], query_rope[0],
        key_up, value_up, grad_out[0],
    )
    lat, key_grad, value_grad = pl.pallas_call(
        widen,
        out_shape=(
            jax.ShapeDtypeStruct((rows, share), BF16),
            jax.ShapeDtypeStruct((width, cols), F32),
            jax.ShapeDtypeStruct((width, cols), F32),
        ),
        in_specs=[hbm] * 3,
        out_specs=(hbm,) * 3,
        scratch_shapes=[
            vmem((rows, share), BF16), vmem((2, width, cols), BF16), vmem((2, width, cols), F32),
            dma((3, CUTS)), dma((3, CUTS)),
        ],
        compiler_params=pltpu.CompilerParams(vmem_limit_bytes=60 * 1024 * 1024),
    )(lat, key_grad, value_grad)
    return lat[None], key_grad, value_grad


def solution(mesh):
    in_specs = (
        P("dp", "ctx", "head"),
        P("dp", "ctx", "head"),
        P("dp", "ctx", None),
        P("dp", "ctx", None),
        P(None, "head"),
        P(None, "head"),
        P("dp", "ctx", "head"),
        P(),
    )
    out_specs = (P("dp", "ctx", "head"), P(None, "head"), P(None, "head"))
    return jax.shard_map(shards, mesh=mesh, in_specs=in_specs, out_specs=out_specs, check_vma=False)
```
